32 devices in a mesh: row: 8 (over z, core), col: 4 (over y, x).
Axes of the slice: x: 2, y: 2, z: 4, core: 2. Of those that a mesh axis runs over, the one named last changes fastest.
Arguments:
- tile_values: float32 [1536, 32, 1024], P(('row', 'col')), may hold values from -6 to 6
- tile_count: int32 [32], P(('row', 'col')), may hold values from 1 to 48, as said below
- mode1_column: int32 [1536, 1], P(('row', 'col')), may hold values from 0 to 3; in each aligned block of 48 rows (0 to 47, 48 to 95, ...) at most 13 rows name the same one
- mode1_offset: int32 [1536], P(('row', 'col')), may hold values from 0 to 15
- mode2_row: int32 [1536, 1], P(('row', 'col')), may hold values from 0 to 7; in each aligned block of 48 rows (0 to 47, 48 to 95, ...) at most 7 rows name the same one
- mode2_offset: int32 [1536], P(('row', 'col')), may hold values from 0 to 7
- mode3_offset: int32 [1536], P(('row', 'col')), may hold values from 0 to 15
- mode2_factor: float32 [8192, 256], P(('row', 'col'))
- mode3_factor: float32 [2048, 256], P('col')
Outputs:
- updated: float32 [16384, 256], P(('row', 'col'))
The draws below stay inside these ranges and needn't reach their ends.
Inputs may be any that keep to these rules, and one draw needn't show every extreme that they name: Device d's live tiles fill its first tile_count[d] slots; other slots are ignored. Some device holds 48 live tiles. `mode1_column`: at most 13 slots of one device name the same value, and some device reaches it. `mode2_row`: at most 7 slots of one device name the same value, and some device reaches it.
All inputs are finite; a program needn't handle non-finite values.
Results may differ from the reference program's by a relative error of at most 0.0003.
Values sent between devices are 32-bit elements; how exact they have to be, the bound alone decides.
A program may use at most 128 MiB of HBM per device.

```python
import math
import jax
import jax.numpy as jnp
import numpy as np
from jax import lax

RANK = 256
TILE = 32
TILES_DEV = 48
IB_DEV = 16
JB_DEV = 8
KB_COL = 16
TILES = 1536
I = 16384
J = 8192
K = 2048
ACAP = 13
BCAP = 7
N_ROW = 8
N_COL = 4
DEVICES = 32


def draw_tile_count(key, part):
    spread_key, busy_key = jax.random.split(jax.random.fold_in(key, 3))
    span_width = max(1, TILES_DEV // 4)
    floor_count = TILES_DEV - span_width
    drawn_values = jax.random.randint(spread_key, (DEVICES,), 0, span_width + 1)
    counts = floor_count + (drawn_values * drawn_values + span_width - 1) // span_width
    busiest = jax.random.randint(busy_key, (), 0, DEVICES)
    return jnp.where(jnp.arange(DEVICES) == busiest, TILES_DEV, counts).astype(jnp.int32)


def draw_factor(key, row_total, salt_value):
    key_list = jax.random.split(jax.random.fold_in(key, salt_value), 4)
    position = jnp.arange(row_total, dtype=jnp.float32)[:, None] / row_total
    rough_scale = jnp.exp(jax.random.uniform(key_list[0], (row_total, 1), jnp.float32, -1.15, 1.15))
    column_scale = jnp.exp(jax.random.uniform(key_list[1], (1, RANK), jnp.float32, 0.0, 1.1))
    shared = jnp.clip(jax.random.normal(key_list[2], (row_total, 1), jnp.float32), -4.0, 4.0)
    ramp_scale = 0.6 + 1.2 * position
    noise_part = jnp.clip(jax.random.normal(key_list[3], (row_total, RANK), jnp.float32), -5.0, 5.0)
    shared_weight = 0.6
    return ramp_scale * rough_scale * column_scale * (noise_part + shared_weight * shared) * (0.5 * math.sqrt(TILE) / row_total)


def draw_mode2_factor(key, part):
    return draw_factor(key, J, 21)


def draw_mode3_factor(key, part):
    return draw_factor(key, K, 22)


def touch_ends(values, own_key, low, top_value):
    place = [jax.random.randint(jax.random.fold_in(own_key, axis), (), 0, length) for axis, length in enumerate(values.shape)]
    longest = values.shape.index(max(values.shape))
    next_to = place[:longest] + [(place[longest] + 1) % values.shape[longest]] + place[longest + 1:]
    return values.at[tuple(place)].set(low).at[tuple(next_to)].set(top_value)


def shard_levels(own_key, dims, cuts, least, high):
    level = 1.0
    for axis_at, parts in cuts:
        steps = jax.random.uniform(jax.random.fold_in(jax.random.fold_in(own_key, 6), axis_at), (parts,), jnp.float32, least / len(cuts), high / len(cuts))
        level = level * jnp.repeat(jnp.exp(steps), dims[axis_at] // parts).reshape((-1,) + (1,) * (len(dims) - 1 - axis_at))
    return level


def assign_block(stream_key, own, number, rows, number_of, top, limit, slope):
    ranking = jax.random.permutation(stream_key, number_of)
    packed, common = load_shares(number_of, rows * top, limit, slope, True), load_shares(number_of, rows * top, limit, slope, False)
    places = jnp.arange(number_of)

    def named(lengths, turn):
        used = int((lengths > 0).sum())
        fixed = max(1, used // 4)
        moved = fixed + (places - fixed + turn * (used - fixed)) % max(1, number_of - fixed)
        return jnp.zeros((number_of,), jnp.int32).at[ranking[jnp.where(places < fixed, places, moved)]].set(jnp.asarray(lengths, jnp.int32))

    lengths = jnp.where(number % 4 == 0, named(packed, number // 4), named(common, number - number // 4 - 1))
    mixed = jax.random.permutation(jax.random.fold_in(own, 3), number_of)
    giver, receiver = mixed[0:number_of // 2 * 2:2], mixed[1:number_of // 2 * 2:2]
    margin = jnp.minimum(lengths[giver] - 1, limit - lengths[receiver]) // 2
    margin = jnp.where((giver == ranking[0]) | (receiver == ranking[0]) | (lengths[receiver] == 0), 0, jnp.maximum(margin, 0))
    moved = jax.random.randint(jax.random.fold_in(own, 4), (number_of // 2,), 0, 1 << 20) % (margin + 1)
    lengths = lengths.at[giver].add(-moved).at[receiver].add(moved)
    labels = jnp.searchsorted(jnp.cumsum(lengths), jnp.arange(rows * top), side="right").astype(jnp.int32)
    table = labels.reshape(top, rows).T
    table = table[jax.random.permutation(jax.random.fold_in(own, 1), rows)]
    turn = jax.random.randint(jax.random.fold_in(own, 2), (rows, 1), 0, top)
    return jnp.take_along_axis(table, (jnp.arange(top)[None, :] + turn) % top, axis=1)


def load_shares(count, total, reach, slope, full):
    weights = [(1 << 20) // math.isqrt(grade ** slope) + 1 for grade in range(1, count + 1)]
    largest = reach if full else min(reach, max(-(-total // count), total * weights[0] // sum(weights)))
    least = 1 if total - largest >= count - 1 else 0
    holding, surplus = [largest] + [least] * (count - 1), total - largest - least * (count - 1)
    while surplus > 0:
        free = [i for i in range(1, count) if holding[i] < largest] or [i for i in range(1, count) if holding[i] < reach]
        whole, left = sum([weights[i] for i in free]), surplus
        for i in free:
            addition = min(reach - holding[i], max(1, left * weights[i] // whole), surplus)
            holding[i] = holding[i] + addition
            surplus = surplus - addition
    return np.array(holding)


def normal_values(rng, extent, width, most, cuts=(), held_as=jnp.bfloat16):
    entries = jax.random.normal(rng, extent, jnp.float32) * width
    if len(cuts) > 0:
        entries = shard_levels(rng, extent, cuts, -0.22, 0.18) * entries
    return jnp.clip(entries, min=-most, max=most).astype(held_as)


def setup_inputs(seed: int = 0) -> dict:
    key_of = jax.random.split(jax.random.key(seed), 10)
    tile_values = normal_values(key_of[0], (TILES, TILE, TILE * TILE), 1.0, 6.0, ((0, 32),), jnp.float32)
    tile_count = draw_tile_count(jax.random.fold_in(key_of[9], 71), 0)
    mode1_column_keys = jax.random.split(jax.random.fold_in(key_of[2], 1), TILES // TILES_DEV)
    mode1_column_turns = jax.random.permutation(jax.random.fold_in(key_of[2], 3), TILES // TILES_DEV)
    mode1_column = jax.vmap(lambda own, number: assign_block(jax.random.fold_in(key_of[2], 2), own, number, TILES_DEV, N_COL, 1, ACAP, 2))(mode1_column_keys, mode1_column_turns).reshape((TILES, 1))
    mode1_offset = touch_ends(jax.random.randint(key_of[3], (TILES,), 0, IB_DEV), jax.random.fold_in(key_of[3], 1), 0, IB_DEV - 1).astype(jnp.int32)
    mode2_row_keys = jax.random.split(jax.random.fold_in(key_of[4], 1), TILES // TILES_DEV)
    mode2_row_turns = jax.random.permutation(jax.random.fold_in(key_of[4], 3), TILES // TILES_DEV)
    mode2_row = jax.vmap(lambda own, number: assign_block(jax.random.fold_in(key_of[4], 2), own, number, TILES_DEV, N_ROW, 1, BCAP, 2))(mode2_row_keys, mode2_row_turns).reshape((TILES, 1))
    mode2_offset = touch_ends(jax.random.randint(key_of[5], (TILES,), 0, JB_DEV), jax.random.fold_in(key_of[5], 1), 0, JB_DEV - 1).astype(jnp.int32)
    mode3_offset = touch_ends(jax.random.randint(key_of[6], (TILES,), 0, KB_COL), jax.random.fold_in(key_of[6], 1), 0, KB_COL - 1).astype(jnp.int32)
    mode2_factor = draw_mode2_factor(jax.random.fold_in(key_of[9], 71), 0)
    mode3_factor = draw_mode3_factor(jax.random.fold_in(key_of[9], 71), 0)
    return {"tile_values": tile_values, "tile_count": tile_count, "mode1_column": mode1_column, "mode1_offset": mode1_offset, "mode2_row": mode2_row, "mode2_offset": mode2_offset, "mode3_offset": mode3_offset, "mode2_factor": mode2_factor, "mode3_factor": mode3_factor}


HIGHEST_PRECISION = lax.Precision.HIGHEST

def product_of(left_matrix, right_matrix):
    return lax.dot_general(left_matrix.astype(jnp.float32), right_matrix.astype(jnp.float32), (((0,), (0,)), ((), ())), precision=HIGHEST_PRECISION, preferred_element_type=jnp.float32)

def reference(tile_values, tile_count, mode1_column, mode1_offset, mode2_row, mode2_offset, mode3_offset, mode2_factor, mode3_factor):
    tile_total = tile_values.shape[0]
    tile_edge = tile_values.shape[1]
    rank_width = mode2_factor.shape[1]
    slot_index = jnp.arange(tile_total, dtype=jnp.int32)
    device_index = slot_index // TILES_DEV
    grid_row = device_index // N_COL
    grid_column = device_index % N_COL
    is_live = slot_index % TILES_DEV < tile_count[device_index]
    mode1_block = ((grid_row * N_COL + mode1_column[:, 0]) * IB_DEV + mode1_offset).astype(jnp.int32)
    mode2_block = ((mode2_row[:, 0] * N_COL + grid_column) * JB_DEV + mode2_offset).astype(jnp.int32)
    mode3_block = (grid_column * KB_COL + mode3_offset).astype(jnp.int32)

    def contribute(slot_at, carried):
        second_rows = lax.dynamic_slice_in_dim(mode2_factor, (mode2_block[slot_at] * tile_edge).astype(jnp.int32), tile_edge, 0)
        third_rows = lax.dynamic_slice_in_dim(mode3_factor, (mode3_block[slot_at] * tile_edge).astype(jnp.int32), tile_edge, 0)
        khatri = (second_rows[:, None, :] * third_rows[None, :, :]).reshape(tile_edge * tile_edge, rank_width)
        product_rows = jnp.dot(tile_values[slot_at].astype(jnp.float32), khatri.astype(jnp.float32), precision=HIGHEST_PRECISION, preferred_element_type=jnp.float32)
        row_start = (mode1_block[slot_at] * tile_edge).astype(jnp.int32)
        current_rows = lax.dynamic_slice_in_dim(carried, row_start, tile_edge, 0)
        return lax.dynamic_update_slice_in_dim(carried, current_rows + product_rows, row_start, 0)

    def visit_slot(slot_at, carried):
        return lax.cond(is_live[slot_at], lambda inner: contribute(slot_at, inner), lambda inner: inner, carried)
    mttkrp = lax.fori_loop(0, tile_total, visit_slot, jnp.zeros((I, rank_width), jnp.float32))
    normal_matrix = product_of(mode2_factor, mode2_factor) * product_of(mode3_factor, mode3_factor)
    cholesky_factor = jnp.linalg.cholesky(normal_matrix)
    return jax.scipy.linalg.cho_solve((cholesky_factor, True), mttkrp.T).T
```

```python
import functools

import jax
import jax.numpy as jnp
from jax import lax
from jax.experimental import pallas as pl
from jax.experimental.pallas import tpu as pltpu
from jax.sharding import PartitionSpec as P

IB_DEV = 16
PIVOT = 32
MESH = pl.DeviceIdType.MESH
HIGHEST = lax.Precision.HIGHEST


def exact_dot(left, right, contract=((1,), (0,))):
    return lax.dot_general(
        left, right, (contract, ((), ())), precision=HIGHEST, preferred_element_type=jnp.float32
    )


def split(values):
    high = values.astype(jnp.bfloat16)
    return high, (values - high.astype(jnp.float32)).astype(jnp.bfloat16)


def invert_small(block):
    size = block.shape[0]
    line = lax.broadcasted_iota(jnp.int32, (size, size), 0)
    lane = lax.broadcasted_iota(jnp.int32, (size, size), 1)
    lane_row = lax.broadcasted_iota(jnp.int32, (1, size), 1)
    for k in range(size):
        scale = 1.0 / block[k : k + 1, k : k + 1]
        row = jnp.where(lane_row == k, scale, block[k : k + 1, :] * scale)
        column = block[:, k : k + 1]
        kept = jnp.where(lane == k, 0.0, block)
        block = jnp.where(line == k, row, kept - column * row)
    return block


def eliminate(matrix, at):
    size = matrix.shape[0]
    start = at * PIVOT
    rows = matrix[start : start + PIVOT, :]
    columns = matrix[:, start : start + PIVOT]
    lane = lax.broadcasted_iota(jnp.int32, (PIVOT, size), 1)
    line = lax.broadcasted_iota(jnp.int32, (PIVOT, size), 0)
    inside = (lane >= start) & (lane < start + PIVOT)
    pivot = invert_small(rows[:, start : start + PIVOT])
    unit = jnp.where(lane - start == line, 1.0, 0.0)
    new_rows = exact_dot(pivot, jnp.where(inside, unit, rows))
    lane_all = lax.broadcasted_iota(jnp.int32, (size, size), 1)
    inside_all = (lane_all >= start) & (lane_all < start + PIVOT)
    rest = jnp.where(inside_all, 0.0, matrix) - exact_dot(columns, new_rows)
    pieces = [rest[:start], new_rows, rest[start + PIVOT :]]
    return jnp.concatenate([piece for piece in pieces if piece.shape[0]], axis=0)


def kernel(
    n_row,
    n_col,
    index_ref,
    live_ref,
    target_ref,
    x_hbm,
    b_ref,
    c_ref,
    out_ref,
    x_ref,
    b_all,
    c_high,
    c_low,
    gram2,
    gram3,
    gram_in,
    normal_in,
    partials,
    send,
    arrive,
    x_sem,
    line_send,
    line_recv,
    pair_send,
    pair_recv,
    gram_send,
    gram_recv,
    normal_send,
    normal_recv,
    block_send,
    block_recv,
):
    row = lax.axis_index("row")
    col = lax.axis_index("col")
    chip, core = row // 2, row % 2
    chips = n_row // 2
    other = chip * 2 + 1 - core
    slots, edge = x_ref.shape[0], x_ref.shape[1]
    rank = b_ref.shape[1]
    piece = rank // n_row
    rows_out = IB_DEV * edge
    held_blocks = b_ref.shape[0] // edge

    load_x = pltpu.make_async_copy(x_hbm, x_ref, x_sem)
    load_x.start()

    barrier = pltpu.get_barrier_semaphore()
    for step in range(1, n_row):
        pl.semaphore_signal(
            barrier, inc=1, device_id=((row + step) % n_row, col), device_id_type=MESH
        )
    for step in range(1, n_col):
        pl.semaphore_signal(
            barrier, inc=1, device_id=(row, (col + step) % n_col), device_id_type=MESH
        )
    b_all[pl.ds(row * held_blocks, held_blocks)] = b_ref[...].reshape(held_blocks, edge, rank)
    pl.semaphore_wait(barrier, n_row + n_col - 2)

    def line_copy(way, step, slot_chip, to_chip):
        held = pl.ds((slot_chip * 2 + core) * held_blocks, held_blocks)
        return pltpu.make_async_remote_copy(
            src_ref=b_all.at[held],
            dst_ref=b_all.at[held],
            send_sem=line_send.at[way, step],
            recv_sem=line_recv.at[way, step],
            device_id=(to_chip * 2 + core, col),
            device_id_type=MESH,
        )

    def pair_copy(number, slot_row):
        held = pl.ds(slot_row * held_blocks, held_blocks)
        return pltpu.make_async_remote_copy(
            src_ref=b_all.at[held],
            dst_ref=b_all.at[held],
            send_sem=pair_send.at[number],
            recv_sem=pair_recv.at[number],
            device_id=(other, col),
            device_id_type=MESH,
        )

    def has(way, step):
        return chip >= 1 + step if way == 0 else chip + 1 + step < chips

    def sends(way, step):
        if way == 0:
            return (chip < chips - 1) & (chip >= step)
        return (chip > 0) & (chip + step < chips)

    def sent_chip(way, step):
        return chip - step if way == 0 else chip + step

    def next_chip(way):
        return chip + 1 if way == 0 else chip - 1

    for way in range(2):

        @pl.when(sends(way, 0))
        def _():
            line_copy(way, 0, sent_chip(way, 0), next_chip(way)).start()

    pair_copy(0, row).start()

    third = c_ref[...]
    high, low = split(third)
    c_high[...] = high.reshape(c_high.shape)
    c_low[...] = low.reshape(c_low.shape)
    gram3[...] = exact_dot(third, third, ((0,), (0,)))
    own = b_ref[...]
    gram2[...] = exact_dot(own, own, ((0,), (0,)))
    pair_copy(0, other).wait_recv()

    def add_gram(slot_row):
        block = b_all[pl.ds(slot_row * held_blocks, held_blocks)].reshape(b_ref.shape)
        gram2[...] += exact_dot(block, block, ((0,), (0,)))

    add_gram(other)
    for step in range(chips - 1):
        for way in range(2):

            @pl.when(has(way, step))
            def _():
                held = sent_chip(way, step + 1)
                line_copy(way, step, held, next_chip(way)).wait_recv()
                pair_copy(1 + 2 * step + way, held * 2 + core).start()

            if step + 1 < chips - 1:

                @pl.when(sends(way, step + 1))
                def _():
                    line_copy(way, step + 1, sent_chip(way, step + 1), next_chip(way)).start()

        for way in range(2):

            @pl.when(has(way, step))
            def _():
                held = sent_chip(way, step + 1)
                add_gram(held * 2 + core)
                pair_copy(1 + 2 * step + way, held * 2 + 1 - core).wait_recv()
                add_gram(held * 2 + 1 - core)

    def gram_copy(step, which):
        to_col = (col + step) % n_col
        source = gram2 if which == 0 else gram3
        return pltpu.make_async_remote_copy(
            src_ref=source.at[pl.ds(pl.multiple_of(row * piece, 8), piece)],
            dst_ref=gram_in.at[which, step],
            send_sem=gram_send.at[which, step],
            recv_sem=gram_recv.at[which, step],
            device_id=(row, to_col),
            device_id_type=MESH,
        )

    for step in range(1, n_col):
        gram_copy(step, 0).start()
        gram_copy(step, 1).start()

    load_x.wait()
    lane = lax.broadcasted_iota(jnp.int32, (edge, 128), 1)
    lane_row = lax.broadcasted_iota(jnp.int32, (1, 128), 1) // edge
    one_mask = [jnp.where(lane_row == m, 1.0, 0.0).astype(jnp.bfloat16) for m in range(4)]
    two_mask = [jnp.where(lane_row % 2 == m, 1.0, 0.0).astype(jnp.bfloat16) for m in range(2)]
    chunks = edge * edge // 128

    def tile(t, carried):
        third_at = index_ref[1, t]
        weights_high = c_high[third_at]
        weights_low = c_low[third_at]
        weights = jnp.concatenate([weights_high] * 6 + [weights_low] * 2, axis=0)
        pieces = []
        for q in range(chunks):
            x = x_ref[t, :, q * 128 : (q + 1) * 128]
            first = x.astype(jnp.bfloat16)
            x_high = first.astype(jnp.float32)
            x_low = x - x_high
            turned_high = pltpu.roll(x_high, 64, 1)
            turned_low = pltpu.roll(x_low, 64, 1)
            front = jnp.where(lane < 64, x_low, turned_high).astype(jnp.bfloat16)
            back = jnp.where(lane < 64, turned_low, x_high).astype(jnp.bfloat16)
            for m in range(4):
                rest = front if m < 2 else back
                pieces.append(
                    jnp.concatenate([first * one_mask[m], rest * two_mask[m % 2]], axis=1)
                )
        inner = jnp.dot(
            jnp.concatenate(pieces, axis=0), weights, preferred_element_type=jnp.float32
        )
        second = b_all[index_ref[0, t]]
        total = inner[:edge] * second[0:1]
        for j in range(1, edge):
            total = total + inner[j * edge : (j + 1) * edge] * second[j : j + 1]
        partials[:, pl.ds(t, 1), :] = total[:, None, :]
        return carried

    lax.fori_loop(0, slots, tile, 0)

    for step in range(1, n_col):
        gram_copy(step, 0).wait_recv()
        gram_copy(step, 1).wait_recv()
    own_piece = pl.ds(pl.multiple_of(row * piece, 8), piece)
    sum2, sum3 = gram2[own_piece, :], gram3[own_piece, :]
    for step in range(1, n_col):
        sum2 = sum2 + gram_in[0, step]
        sum3 = sum3 + gram_in[1, step]
    normal_in[row] = sum2 * sum3

    def normal_copy(step, slot):
        return pltpu.make_async_remote_copy(
            src_ref=normal_in.at[slot],
            dst_ref=normal_in.at[slot],
            send_sem=normal_send.at[step],
            recv_sem=normal_recv.at[step],
            device_id=((row + step) % n_row, col),
            device_id_type=MESH,
        )

    for step in range(1, n_row):
        normal_copy(step, row).start()

    targets = n_col * IB_DEV
    chosen = lax.broadcasted_iota(jnp.int32, (targets, slots), 0) == target_ref[...]
    chosen = jnp.where(chosen, 1.0, 0.0)
    chosen = jnp.concatenate([chosen, chosen], axis=1).astype(jnp.bfloat16)

    live = live_ref[...] > 0

    def choose(i, carried):
        high, low = split(jnp.where(live, partials[i], 0.0))
        rows = jnp.dot(
            chosen, jnp.concatenate([high, low], axis=0), preferred_element_type=jnp.float32
        )
        for c in range(n_col):
            send[c, pl.ds(pl.multiple_of(i * IB_DEV, IB_DEV), IB_DEV), :] = rows[
                c * IB_DEV : (c + 1) * IB_DEV
            ]
        return carried

    lax.fori_loop(0, edge, choose, 0)

    def block_copy(number, source, target, to_col):
        return pltpu.make_async_remote_copy(
            src_ref=source,
            dst_ref=target,
            send_sem=block_send.at[number],
            recv_sem=block_recv.at[number],
            device_id=(row, to_col),
            device_id_type=MESH,
        )

    half = rows_out // 2
    halves = (pl.ds(0, half), pl.ds(half, half))
    copies = []
    later = []
    if n_col == 4:
        near = (col // 2) * 2 + 1 - col % 2
        far = (1 - col // 2) * 2 + col % 2
        corner = (1 - col // 2) * 2 + 1 - col % 2
        sides = (near, far)
        for way in range(2):
            copies.append(
                block_copy(way, send.at[corner, halves[way]], arrive.at[0, halves[way]], sides[way])
            )
        for way in range(2):
            copies.append(
                block_copy(2 + way, send.at[sides[way], halves[way]], arrive.at[1, halves[way]], sides[way])
            )
        for way in range(2):
            later.append(
                block_copy(4 + way, send.at[sides[1 - way], halves[way]], arrive.at[2, halves[way]], sides[1 - way])
            )
    else:
        for step in range(1, n_col):
            to_col = (col + step) % n_col
            copies.append(block_copy(step - 1, send.at[to_col], arrive.at[step - 1], to_col))
    for copy in copies:
        copy.start()

    for step in range(1, n_row):
        normal_copy(step, (row + n_row - step) % n_row).wait_recv()
    matrix = jnp.concatenate([normal_in[r] for r in range(n_row)], axis=0)
    pivots = rank // PIVOT
    for at in range(pivots // 2):
        matrix = eliminate(matrix, at)
    if later:
        for way in range(2):
            copies[way].wait_recv()
            send[sides[1 - way], halves[way]] += arrive[0, halves[way]]
            later[way].start()
    for at in range(pivots // 2, pivots):
        matrix = eliminate(matrix, at)

    total = send[col]
    if later:
        for copy in copies[2:] + later:
            copy.wait_recv()
        total = total + arrive[1] + arrive[2]
    else:
        for copy in copies:
            copy.wait_recv()
        for step in range(n_col - 1):
            total = total + arrive[step]
    solved = exact_dot(total, matrix)
    for i in range(edge):
        out_ref[:, i : i + 1, :] = solved[i * IB_DEV : (i + 1) * IB_DEV][:, None, :]

    for copy in copies + later:
        copy.wait_send()
    for step in range(1, n_row):
        normal_copy(step, row).wait_send()
    for step in range(1, n_col):
        gram_copy(step, 0).wait_send()
        gram_copy(step, 1).wait_send()
    pair_copy(0, row).wait_send()
    for step in range(chips - 1):
        for way in range(2):

            @pl.when(has(way, step))
            def _():
                pair_copy(1 + 2 * step + way, sent_chip(way, step + 1) * 2 + core).wait_send()

            @pl.when(sends(way, step))
            def _():
                line_copy(way, step, sent_chip(way, step), next_chip(way)).wait_send()


def local(
    n_row,
    n_col,
    tile_values,
    tile_count,
    mode1_column,
    mode1_offset,
    mode2_row,
    mode2_offset,
    mode3_offset,
    mode2_factor,
    mode3_factor,
):
    slots, edge = tile_values.shape[0], tile_values.shape[1]
    rows_held, rank = mode2_factor.shape
    blocks_held = rows_held // edge
    is_live = jnp.arange(slots, dtype=jnp.int32) < tile_count[0]
    index = jnp.stack([mode2_row[:, 0] * blocks_held + mode2_offset, mode3_offset])
    target = jnp.where(is_live, mode1_column[:, 0] * IB_DEV + mode1_offset, -1)[None, :]
    live = is_live.astype(jnp.int32)[:, None]
    rows_out = IB_DEV * edge
    piece = rank // n_row
    chips = n_row // 2
    f32, bf16 = jnp.float32, jnp.bfloat16
    dma = pltpu.SemaphoreType.DMA
    vmem = pl.BlockSpec(memory_space=pltpu.VMEM)
    smem = pl.BlockSpec(memory_space=pltpu.SMEM)
    blocks = max(6, n_col - 1)
    out = pl.pallas_call(
        functools.partial(kernel, n_row, n_col),
        out_shape=jax.ShapeDtypeStruct((IB_DEV, edge, rank), f32),
        in_specs=[smem, vmem, vmem, pl.BlockSpec(memory_space=pl.ANY), vmem, vmem],
        out_specs=vmem,
        scratch_shapes=[
            pltpu.VMEM(tile_values.shape, f32),
            pltpu.VMEM((n_row * blocks_held, edge, rank), f32),
            pltpu.VMEM((mode3_factor.shape[0] // edge, edge, rank), bf16),
            pltpu.VMEM((mode3_factor.shape[0] // edge, edge, rank), bf16),
            pltpu.VMEM((rank, rank), f32),
            pltpu.VMEM((rank, rank), f32),
            pltpu.VMEM((2, n_col, piece, rank), f32),
            pltpu.VMEM((n_row, piece, rank), f32),
            pltpu.VMEM((edge, slots, rank), f32),
            pltpu.VMEM((n_col, rows_out, rank), f32),
            pltpu.VMEM((max(3, n_col - 1), rows_out, rank), f32),
            dma,
            dma((2, chips)),
            dma((2, chips)),
            dma((2 * chips,)),
            dma((2 * chips,)),
            dma((2, n_col)),
            dma((2, n_col)),
            dma((n_row,)),
            dma((n_row,)),
            dma((blocks,)),
            dma((blocks,)),
        ],
        compiler_params=pltpu.CompilerParams(
            collective_id=0, has_side_effects=True, vmem_limit_bytes=52 * 2**20
        ),
    )(index, live, target, tile_values, mode2_factor, mode3_factor)
    return out.reshape(rows_out, rank)


def solution(mesh):
    placed = (
        P(("row", "col"), None, None),
        P(("row", "col")),
        P(("row", "col"), None),
        P(("row", "col")),
        P(("row", "col"), None),
        P(("row", "col")),
        P(("row", "col")),
        P(("row", "col"), None),
        P("col", None),
    )
    return jax.shard_map(
        functools.partial(local, mesh.shape["row"], mesh.shape["col"]),
        mesh=mesh,
        in_specs=placed,
        out_specs=P(("row", "col"), None),
        check_vma=False,
    )
```

```python
import functools

import jax
import jax.numpy as jnp
from jax import lax
from jax.experimental import pallas as pl
from jax.experimental.pallas import tpu as pltpu
from jax.sharding import PartitionSpec as P

IB_DEV = 16
PIVOT = 32
MESH = pl.DeviceIdType.MESH
HIGHEST = lax.Precision.HIGHEST


def exact_dot(left, right, contract=((1,), (0,))):
    return lax.dot_general(
        left, right, (contract, ((), ())), precision=HIGHEST, preferred_element_type=jnp.float32
    )


def split(values):
    high = values.astype(jnp.bfloat16)
    return high, (values - high.astype(jnp.float32)).astype(jnp.bfloat16)


def split_three(values):
    high = values.astype(jnp.bfloat16)
    rest = values - high.astype(jnp.float32)
    middle = rest.astype(jnp.bfloat16)
    return high, middle, (rest - middle.astype(jnp.float32)).astype(jnp.bfloat16)


def invert_small(block):
    size = block.shape[0]
    line = lax.broadcasted_iota(jnp.int32, (size, size), 0)
    lane = lax.broadcasted_iota(jnp.int32, (size, size), 1)
    lane_row = lax.broadcasted_iota(jnp.int32, (1, size), 1)
    for k in range(size):
        column = jnp.broadcast_to(block[:, k : k + 1], (size, size))
        scale = 1.0 / column[k : k + 1, :]
        row = jnp.where(lane_row == k, scale, block[k : k + 1, :] * scale)
        kept = jnp.where(lane == k, 0.0, block)
        block = jnp.where(line == k, row, kept - column * row)
    return block


def eliminate(matrix, at):
    size = matrix.shape[0]
    start = at * PIVOT
    rows = matrix[start : start + PIVOT, :]
    lane = lax.broadcasted_iota(jnp.int32, (PIVOT, size), 1)
    line = lax.broadcasted_iota(jnp.int32, (PIVOT, size), 0)
    inside = (lane >= start) & (lane < start + PIVOT)
    pivot = invert_small(rows[:, start : start + PIVOT])
    unit = jnp.where(lane - start == line, 1.0, 0.0)
    high, middle, low = split_three(jnp.where(inside, unit, rows))
    p_high, p_middle, p_low = split_three(pivot)
    new_rows = jnp.dot(
        jnp.concatenate([p_high, p_high, p_middle, p_high, p_middle, p_low], axis=1),
        jnp.concatenate([high, middle, high, low, middle, high], axis=0),
        preferred_element_type=jnp.float32,
    )
    c_high, c_middle, c_low = split_three(jnp.where(lane < start, -rows, rows))
    high, middle, low = split_three(new_rows)
    change = lax.dot_general(
        jnp.concatenate([c_high, c_high, c_middle, c_high, c_middle, c_low], axis=0),
        jnp.concatenate([high, middle, high, low, middle, high], axis=0),
        (((0,), (0,)), ((), ())),
        preferred_element_type=jnp.float32,
    )
    lane_all = lax.broadcasted_iota(jnp.int32, (size, size), 1)
    inside_all = (lane_all >= start) & (lane_all < start + PIVOT)
    rest = jnp.where(inside_all, 0.0, matrix) - change
    pieces = [rest[:start], new_rows, rest[start + PIVOT :]]
    return jnp.concatenate([piece for piece in pieces if piece.shape[0]], axis=0)


def kernel(
    n_row,
    n_col,
    row_most,
    count_ref,
    lists_ref,
    x_hbm,
    b_hbm,
    c_hbm,
    out_ref,
    lists,
    index_ref,
    x_ref,
    b_all,
    b_now,
    c_ref,
    c_high,
    c_low,
    gram2,
    gram3,
    gram_in,
    normal_in,
    partials,
    send,
    arrive,
    load_sem,
    line_send,
    line_recv,
    pair_send,
    pair_recv,
    gram_send,
    gram_recv,
    normal_send,
    normal_recv,
    block_send,
    block_recv,
):
    row = lax.axis_index("row")
    col = lax.axis_index("col")
    chip, core = row // 2, row % 2
    chips = n_row // 2
    other = chip * 2 + 1 - core
    edge = x_ref.shape[1]
    slots = lists.shape[0]
    per_row = row_most
    rank = c_ref.shape[1]
    piece = rank // n_row
    rows_out = IB_DEV * edge
    held_blocks = b_hbm.shape[0]
    own_blocks = pl.ds(row * held_blocks, held_blocks)

    load_b = pltpu.make_async_copy(b_hbm, b_all.at[own_blocks], load_sem.at[0])
    load_c = pltpu.make_async_copy(c_hbm, c_ref, load_sem.at[1])
    load_x = pltpu.make_async_copy(x_hbm, x_ref, load_sem.at[2])
    load_b.start()
    load_c.start()
    load_x.start()

    barrier = pltpu.get_barrier_semaphore()
    for step in range(1, n_row):
        pl.semaphore_signal(
            barrier, inc=1, device_id=((row + step) % n_row, col), device_id_type=MESH
        )
    for step in range(1, n_col):
        pl.semaphore_signal(
            barrier, inc=1, device_id=(row, (col + step) % n_col), device_id_type=MESH
        )
    tiles = lists_ref.shape[1]
    tile_line = lax.broadcasted_iota(jnp.int32, (tiles, tiles), 0)
    tile_lane = lax.broadcasted_iota(jnp.int32, (tiles, tiles), 1)
    owner = lists_ref[0:1, :]
    owner_line = jnp.sum(
        jnp.where(tile_line == tile_lane, owner, 0), axis=1, keepdims=True, dtype=jnp.int32
    )
    before = (owner_line == owner) & (tile_line < tile_lane)
    place = owner * row_most + jnp.sum(
        jnp.where(before, 1, 0), axis=0, keepdims=True, dtype=jnp.int32
    )
    taken = lax.broadcasted_iota(jnp.int32, (slots, tiles), 0) == place
    number = lax.broadcasted_iota(jnp.int32, (1, tiles), 1)
    code = jnp.where(number < count_ref[0], lists_ref[3:4, :] * IB_DEV + lists_ref[4:5, :] + 1, 0)
    list_lane = lax.broadcasted_iota(jnp.int32, lists.shape, 1)
    table = jnp.zeros(lists.shape, jnp.int32)
    for which, values in enumerate((number, lists_ref[1:2, :], lists_ref[2:3, :], code)):
        listed = jnp.sum(jnp.where(taken, values, 0), axis=1, keepdims=True, dtype=jnp.int32)
        table = jnp.where(list_lane == which, listed, table)
    lists[...] = table
    load_lists = pltpu.make_async_copy(lists, index_ref, load_sem.at[3])
    load_lists.start()

    load_b.wait()
    pl.semaphore_wait(barrier, n_row + n_col - 2)

    def line_copy(way, step, slot_chip, to_chip):
        held = pl.ds((slot_chip * 2 + core) * held_blocks, held_blocks)
        return pltpu.make_async_remote_copy(
            src_ref=b_all.at[held],
            dst_ref=b_all.at[held],
            send_sem=line_send.at[way, step],
            recv_sem=line_recv.at[way, step],
            device_id=(to_chip * 2 + core, col),
            device_id_type=MESH,
        )

    def pair_copy(number, slot_row):
        held = pl.ds(slot_row * held_blocks, held_blocks)
        return pltpu.make_async_remote_copy(
            src_ref=b_all.at[held],
            dst_ref=b_all.at[held],
            send_sem=pair_send.at[number],
            recv_sem=pair_recv.at[number],
            device_id=(other, col),
            device_id_type=MESH,
        )

    def has(way, step):
        return chip >= 1 + step if way == 0 else chip + 1 + step < chips

    def sends(way, step):
        if way == 0:
            return (chip < chips - 1) & (chip >= step)
        return (chip > 0) & (chip + step < chips)

    def sent_chip(way, step):
        return chip - step if way == 0 else chip + step

    def next_chip(way):
        return chip + 1 if way == 0 else chip - 1

    for way in range(2):

        @pl.when(sends(way, 0))
        def _():
            line_copy(way, 0, sent_chip(way, 0), next_chip(way)).start()

    pair_copy(0, row).start()

    load_c.wait()
    third = c_ref[...]
    high, low = split(third)
    c_high[...] = high.reshape(c_high.shape)
    c_low[...] = low.reshape(c_low.shape)
    gram3[...] = exact_dot(third, third, ((0,), (0,)))
    gram2[...] = jnp.zeros_like(gram2)
    load_x.wait()
    load_lists.wait()
    lane = lax.broadcasted_iota(jnp.int32, (edge, 128), 1)
    lane_row = lax.broadcasted_iota(jnp.int32, (1, 128), 1) // edge
    one_mask = [jnp.where(lane_row == m, 1.0, 0.0).astype(jnp.bfloat16) for m in range(4)]
    two_mask = [jnp.where(lane_row % 2 == m, 1.0, 0.0).astype(jnp.bfloat16) for m in range(2)]
    chunks = edge * edge // 128

    def tile(slot, second):
        third_at = index_ref[slot, 2]
        tile_at = index_ref[slot, 0]
        weights = jnp.concatenate([c_high[third_at]] * 6 + [c_low[third_at]] * 2, axis=0)
        pieces = []
        for q in range(chunks):
            x = x_ref[tile_at, :, q * 128 : (q + 1) * 128]
            first = x.astype(jnp.bfloat16)
            x_high = first.astype(jnp.float32)
            x_low = x - x_high
            turned_high = pltpu.roll(x_high, 64, 1)
            turned_low = pltpu.roll(x_low, 64, 1)
            front = jnp.where(lane < 64, x_low, turned_high).astype(jnp.bfloat16)
            back = jnp.where(lane < 64, turned_low, x_high).astype(jnp.bfloat16)
            for m in range(4):
                rest = front if m < 2 else back
                pieces.append(
                    jnp.concatenate([first * one_mask[m], rest * two_mask[m % 2]], axis=1)
                )
        inner = jnp.dot(
            jnp.concatenate(pieces, axis=0), weights, preferred_element_type=jnp.float32
        )
        total = inner[:edge] * second[0:1]
        for j in range(1, edge):
            total = total + inner[j * edge : (j + 1) * edge] * second[j : j + 1]
        partials[:, pl.ds(slot, 1), :] = total[:, None, :]

    def use(held_chip):
        for side in range(2):
            held = b_all[pl.ds((held_chip * 2 + side) * held_blocks, held_blocks)]
            b_now[side] = held
            flat = held.reshape(held_blocks * edge, rank)
            gram2[...] += exact_dot(flat, flat, ((0,), (0,)))

    def tiles_of(held_chip):
        def pair(s, carried):
            for side in range(2):
                slot = (held_chip * 2 + side) * per_row + s
                tile(slot, b_now[side, index_ref[slot, 1]])
            return carried

        lax.fori_loop(0, per_row, pair, 0)

    def gram_copy(step, which):
        to_col = (col + step) % n_col
        source = gram2 if which == 0 else gram3
        return pltpu.make_async_remote_copy(
            src_ref=source.at[pl.ds(pl.multiple_of(row * piece, 8), piece)],
            dst_ref=gram_in.at[which, step],
            send_sem=gram_send.at[which, step],
            recv_sem=gram_recv.at[which, step],
            device_id=(row, to_col),
            device_id_type=MESH,
        )

    nearer = jnp.minimum(chip, chips - 1 - chip)

    def turn(number, carried):
        step = number - 1
        for way in range(2):

            @pl.when((number > 0) & has(way, step))
            def _():
                held = sent_chip(way, step + 1)
                line_copy(way, step, held, next_chip(way)).wait_recv()

                @pl.when((step + 1 < chips - 1) & sends(way, step + 1))
                def _():
                    line_copy(way, step + 1, held, next_chip(way)).start()

                pair_copy(1 + 2 * step + way, held * 2 + core).start()

        both = jnp.where(number % 2 == 1, chip - (number + 1) // 2, chip + number // 2)
        one = jnp.where(
            chip < chips - 1 - chip, chip + number - nearer, chip - number + nearer
        )
        held = jnp.where(number <= 2 * nearer, both, one)
        pair_at = jnp.where(held < chip, 2 * (chip - held) - 1, 2 * (held - chip))
        pair_copy(pair_at, held * 2 + 1 - core).wait_recv()
        use(held)

        @pl.when(number == chips - 1)
        def _():
            for to_step in range(1, n_col):
                gram_copy(to_step, 0).start()
                gram_copy(to_step, 1).start()

        tiles_of(held)
        return carried

    lax.fori_loop(0, chips, turn, 0)

    for step in range(1, n_col):
        gram_copy(step, 0).wait_recv()
        gram_copy(step, 1).wait_recv()
    own_piece = pl.ds(pl.multiple_of(row * piece, 8), piece)
    sum2, sum3 = gram2[own_piece, :], gram3[own_piece, :]
    for step in range(1, n_col):
        sum2 = sum2 + gram_in[0, step]
        sum3 = sum3 + gram_in[1, step]
    normal_in[row] = sum2 * sum3

    def normal_copy(step, slot):
        return pltpu.make_async_remote_copy(
            src_ref=normal_in.at[slot],
            dst_ref=normal_in.at[slot],
            send_sem=normal_send.at[step],
            recv_sem=normal_recv.at[step],
            device_id=((row + step) % n_row, col),
            device_id_type=MESH,
        )

    for step in range(1, n_row):
        normal_copy(step, row).start()

    targets = n_col * IB_DEV
    code_line = lists[:, 3:4]
    same = lax.broadcasted_iota(jnp.int32, (slots, slots), 0) == lax.broadcasted_iota(
        jnp.int32, (slots, slots), 1
    )
    code_lane = jnp.sum(jnp.where(same, code_line, 0), axis=0, keepdims=True, dtype=jnp.int32)
    chosen = lax.broadcasted_iota(jnp.int32, (targets, slots), 0) + 1 == code_lane
    chosen = jnp.where(chosen, 1.0, 0.0)
    chosen = jnp.concatenate([chosen, chosen], axis=1).astype(jnp.bfloat16)

    live = code_line > 0

    def choose(group, carried):
        for part in range(4):
            i = group * 4 + part
            high, low = split(jnp.where(live, partials[i], 0.0))
            rows = jnp.dot(
                chosen, jnp.concatenate([high, low], axis=0), preferred_element_type=jnp.float32
            )
            for c in range(n_col):
                send[c, pl.ds(pl.multiple_of(i * IB_DEV, IB_DEV), IB_DEV), :] = rows[
                    c * IB_DEV : (c + 1) * IB_DEV
                ]
        return carried

    lax.fori_loop(0, edge // 4, choose, 0)

    def block_copy(number, source, target, to_col):
        return pltpu.make_async_remote_copy(
            src_ref=source,
            dst_ref=target,
            send_sem=block_send.at[number],
            recv_sem=block_recv.at[number],
            device_id=(row, to_col),
            device_id_type=MESH,
        )

    half = rows_out // 2
    halves = (pl.ds(0, half), pl.ds(half, half))
    copies = []
    later = []
    if n_col == 4:
        near = (col // 2) * 2 + 1 - col % 2
        far = (1 - col // 2) * 2 + col % 2
        corner = (1 - col // 2) * 2 + 1 - col % 2
        sides = (near, far)
        for way in range(2):
            copies.append(
                block_copy(way, send.at[corner, halves[way]], arrive.at[0, halves[way]], sides[way])
            )
        for way in range(2):
            copies.append(
                block_copy(2 + way, send.at[sides[way], halves[way]], arrive.at[1, halves[way]], sides[way])
            )
        for way in range(2):
            later.append(
                block_copy(4 + way, send.at[sides[1 - way], halves[way]], arrive.at[2, halves[way]], sides[1 - way])
            )
    else:
        for step in range(1, n_col):
            to_col = (col + step) % n_col
            copies.append(block_copy(step - 1, send.at[to_col], arrive.at[step - 1], to_col))
    for copy in copies:
        copy.start()

    for step in range(1, n_row):
        normal_copy(step, (row + n_row - step) % n_row).wait_recv()
    matrix = jnp.concatenate([normal_in[r] for r in range(n_row)], axis=0)
    pivots = rank // PIVOT
    early = 3 * pivots // 8
    for at in range(early):
        matrix = eliminate(matrix, at)
    if later:
        for way in range(2):
            copies[way].wait_recv()
            send[sides[1 - way], halves[way]] += arrive[0, halves[way]]
            later[way].start()
    for at in range(early, pivots):
        matrix = eliminate(matrix, at)

    total = send[col]
    if later:
        for copy in copies[2:] + later:
            copy.wait_recv()
        total = total + arrive[1] + arrive[2]
    else:
        for copy in copies:
            copy.wait_recv()
        for step in range(n_col - 1):
            total = total + arrive[step]
    solved = exact_dot(total, matrix)
    for i in range(edge):
        out_ref[:, i : i + 1, :] = solved[i * IB_DEV : (i + 1) * IB_DEV][:, None, :]

    for copy in copies + later:
        copy.wait_send()
    for step in range(1, n_row):
        normal_copy(step, row).wait_send()
    for step in range(1, n_col):
        gram_copy(step, 0).wait_send()
        gram_copy(step, 1).wait_send()
    pair_copy(0, row).wait_send()
    for step in range(chips - 1):
        for way in range(2):

            @pl.when(has(way, step))
            def _():
                pair_copy(1 + 2 * step + way, sent_chip(way, step + 1) * 2 + core).wait_send()

            @pl.when(sends(way, step))
            def _():
                line_copy(way, step, sent_chip(way, step), next_chip(way)).wait_send()


def local(
    n_row,
    n_col,
    tile_values,
    tile_count,
    mode1_column,
    mode1_offset,
    mode2_row,
    mode2_offset,
    mode3_offset,
    mode2_factor,
    mode3_factor,
):
    slots, edge = tile_values.shape[0], tile_values.shape[1]
    rows_held, rank = mode2_factor.shape
    blocks_held = rows_held // edge
    row_most = {8: 7, 16: 4}.get(n_row, slots)
    places = n_row * row_most
    lists = jnp.stack(
        [mode2_row[:, 0], mode2_offset, mode3_offset, mode1_column[:, 0], mode1_offset]
    )
    rows_out = IB_DEV * edge
    piece = rank // n_row
    chips = n_row // 2
    f32, bf16 = jnp.float32, jnp.bfloat16
    dma = pltpu.SemaphoreType.DMA
    vmem = pl.BlockSpec(memory_space=pltpu.VMEM)
    smem = pl.BlockSpec(memory_space=pltpu.SMEM)
    hbm = pl.BlockSpec(memory_space=pltpu.HBM)
    blocks = max(6, n_col - 1)
    out = pl.pallas_call(
        functools.partial(kernel, n_row, n_col, row_most),
        out_shape=jax.ShapeDtypeStruct((IB_DEV, edge, rank), f32),
        in_specs=[smem, vmem, hbm, hbm, hbm],
        out_specs=vmem,
        scratch_shapes=[
            pltpu.VMEM((places, 128), jnp.int32),
            pltpu.SMEM((places, 128), jnp.int32),
            pltpu.VMEM(tile_values.shape, f32),
            pltpu.VMEM((n_row * blocks_held, edge, rank), f32),
            pltpu.VMEM((2, blocks_held, edge, rank), f32),
            pltpu.VMEM(mode3_factor.shape, f32),
            pltpu.VMEM((mode3_factor.shape[0] // edge, edge, rank), bf16),
            pltpu.VMEM((mode3_factor.shape[0] // edge, edge, rank), bf16),
            pltpu.VMEM((rank, rank), f32),
            pltpu.VMEM((rank, rank), f32),
            pltpu.VMEM((2, n_col, piece, rank), f32),
            pltpu.VMEM((n_row, piece, rank), f32),
            pltpu.VMEM((edge, places, rank), f32),
            pltpu.VMEM((n_col, rows_out, rank), f32),
            pltpu.VMEM((max(3, n_col - 1), rows_out, rank), f32),
            dma((4,)),
            dma((2, chips)),
            dma((2, chips)),
            dma((2 * chips,)),
            dma((2 * chips,)),
            dma((2, n_col)),
            dma((2, n_col)),
            dma((n_row,)),
            dma((n_row,)),
            dma((blocks,)),
            dma((blocks,)),
        ],
        compiler_params=pltpu.CompilerParams(
            collective_id=0, has_side_effects=True, vmem_limit_bytes=60 * 2**20
        ),
    )(tile_count, lists, tile_values, mode2_factor.reshape(blocks_held, edge, rank), mode3_factor)
    return out.reshape(rows_out, rank)


def solution(mesh):
    placed = (
        P(("row", "col"), None, None),
        P(("row", "col")),
        P(("row", "col"), None),
        P(("row", "col")),
        P(("row", "col"), None),
        P(("row", "col")),
        P(("row", "col")),
        P(("row", "col"), None),
        P("col", None),
    )
    return jax.shard_map(
        functools.partial(local, mesh.shape["row"], mesh.shape["col"]),
        mesh=mesh,
        in_specs=placed,
        out_specs=P(("row", "col"), None),
        check_vma=False,
    )
```

```python
import functools

import jax
import jax.numpy as jnp
from jax import lax
from jax.experimental import pallas as pl
from jax.experimental.pallas import tpu as pltpu
from jax.sharding import PartitionSpec as P

IB_DEV = 16
PIVOT = 32
SPREAD = 8
MESH = pl.DeviceIdType.MESH
HIGHEST = lax.Precision.HIGHEST


def exact_dot(left, right, contract=((1,), (0,))):
    return lax.dot_general(
        left, right, (contract, ((), ())), precision=HIGHEST, preferred_element_type=jnp.float32
    )


def split(values):
    high = values.astype(jnp.bfloat16)
    return high, (values - high.astype(jnp.float32)).astype(jnp.bfloat16)


def split_three(values):
    high = values.astype(jnp.bfloat16)
    rest = values - high.astype(jnp.float32)
    middle = rest.astype(jnp.bfloat16)
    return high, middle, (rest - middle.astype(jnp.float32)).astype(jnp.bfloat16)


def invert_small(block):
    size = block.shape[0]
    line = lax.broadcasted_iota(jnp.int32, (size, size), 0)
    lane = lax.broadcasted_iota(jnp.int32, (size, size), 1)
    lane_row = lax.broadcasted_iota(jnp.int32, (1, size), 1)
    for first in range(0, size, SPREAD):
        columns = [
            jnp.broadcast_to(block[:, k : k + 1], (size, size))
            for k in range(first, first + SPREAD)
        ]
        for k in range(first, first + SPREAD):
            column = columns[k - first]
            scale = 1.0 / column[k : k + 1, :]
            row = jnp.where(lane_row == k, scale, block[k : k + 1, :] * scale)
            kept = jnp.where(lane == k, 0.0, block)
            block = jnp.where(line == k, row, kept - column * row)
            for later in range(k + 1 - first, SPREAD):
                entry = columns[later][k : k + 1, :] * scale
                columns[later] = jnp.where(line == k, entry, columns[later] - column * entry)
    return block


def eliminate(matrix, rows, at):
    size = matrix.shape[0]
    start = at * PIVOT
    lane = lax.broadcasted_iota(jnp.int32, (PIVOT, size), 1)
    line = lax.broadcasted_iota(jnp.int32, (PIVOT, size), 0)
    inside = (lane >= start) & (lane < start + PIVOT)
    pivot = invert_small(rows[:, start : start + PIVOT])
    unit = jnp.where(lane - start == line, 1.0, 0.0)
    high, middle, low = split_three(jnp.where(inside, unit, rows))
    p_high, p_middle, p_low = split_three(pivot)
    new_rows = jnp.dot(
        jnp.concatenate([p_high, p_high, p_middle, p_high, p_middle, p_low], axis=1),
        jnp.concatenate([high, middle, high, low, middle, high], axis=0),
        preferred_element_type=jnp.float32,
    )
    c_high, c_middle, c_low = split_three(jnp.where(lane < start, -rows, rows))
    high, middle, low = split_three(new_rows)
    left = jnp.concatenate([c_high, c_high, c_middle, c_high, c_middle, c_low], axis=0)
    right = jnp.concatenate([high, middle, high, low, middle, high], axis=0)

    def change(part):
        return lax.dot_general(
            part, right, (((0,), (0,)), ((), ())), preferred_element_type=jnp.float32
        )

    after = start + PIVOT
    next_rows = None
    if after < size:
        next_rows = jnp.where(inside, 0.0, matrix[after : after + PIVOT]) - change(
            left[:, after : after + PIVOT]
        )
    lane_all = lax.broadcasted_iota(jnp.int32, (size, size), 1)
    inside_all = (lane_all >= start) & (lane_all < after)
    rest = jnp.where(inside_all, 0.0, matrix) - change(left)
    pieces = [rest[:start], new_rows, rest[after:]]
    matrix = jnp.concatenate([piece for piece in pieces if piece.shape[0]], axis=0)
    return matrix, next_rows


def add_squares(squares, mixed, values):
    high, middle = split(values)
    contract = (((0,), (0,)), ((), ()))
    both = lax.dot_general(
        high, jnp.concatenate([high, middle], axis=1), contract, preferred_element_type=jnp.float32
    )
    rest = lax.dot_general(middle, middle, contract, preferred_element_type=jnp.float32)
    width = values.shape[1]
    squares[...] += both[:, :width] + rest
    mixed[...] += both[:, width:]


def kernel(
    n_row,
    n_col,
    row_most,
    count_ref,
    lists_ref,
    x_hbm,
    b_hbm,
    c_hbm,
    out_ref,
    lists,
    index_ref,
    x_ref,
    b_all,
    b_now,
    c_ref,
    c_high,
    c_low,
    gram2,
    gram3,
    mixed,
    gram_in,
    normal_in,
    partials,
    send,
    arrive,
    load_sem,
    line_send,
    line_recv,
    pair_send,
    pair_recv,
    gram_send,
    gram_recv,
    normal_send,
    normal_recv,
    block_send,
    block_recv,
):
    row = lax.axis_index("row")
    col = lax.axis_index("col")
    chip, core = row // 2, row % 2
    chips = n_row // 2
    other = chip * 2 + 1 - core
    edge = x_ref.shape[1]
    slots = lists.shape[0]
    per_row = row_most
    rank = c_ref.shape[1]
    piece = rank // n_row
    rows_out = IB_DEV * edge
    held_blocks = b_hbm.shape[0]
    own_blocks = pl.ds(row * held_blocks, held_blocks)

    load_b = pltpu.make_async_copy(b_hbm, b_all.at[own_blocks], load_sem.at[0])
    load_c = pltpu.make_async_copy(c_hbm, c_ref, load_sem.at[1])
    load_x = pltpu.make_async_copy(x_hbm, x_ref, load_sem.at[2])
    load_b.start()
    load_c.start()
    load_x.start()

    barrier = pltpu.get_barrier_semaphore()
    for step in range(1, n_row):
        pl.semaphore_signal(
            barrier, inc=1, device_id=((row + step) % n_row, col), device_id_type=MESH
        )
    for step in range(1, n_col):
        pl.semaphore_signal(
            barrier, inc=1, device_id=(row, (col + step) % n_col), device_id_type=MESH
        )
    tiles = lists_ref.shape[1]
    tile_line = lax.broadcasted_iota(jnp.int32, (tiles, tiles), 0)
    tile_lane = lax.broadcasted_iota(jnp.int32, (tiles, tiles), 1)
    owner = lists_ref[0:1, :]
    owner_line = jnp.sum(
        jnp.where(tile_line == tile_lane, owner, 0), axis=1, keepdims=True, dtype=jnp.int32
    )
    before = (owner_line == owner) & (tile_line < tile_lane)
    place = owner * row_most + jnp.sum(
        jnp.where(before, 1, 0), axis=0, keepdims=True, dtype=jnp.int32
    )
    taken = lax.broadcasted_iota(jnp.int32, (slots, tiles), 0) == place
    number = lax.broadcasted_iota(jnp.int32, (1, tiles), 1)
    code = jnp.where(number < count_ref[0], lists_ref[3:4, :] * IB_DEV + lists_ref[4:5, :] + 1, 0)
    list_lane = lax.broadcasted_iota(jnp.int32, lists.shape, 1)
    table = jnp.zeros(lists.shape, jnp.int32)
    for which, values in enumerate((number, lists_ref[1:2, :], lists_ref[2:3, :], code)):
        listed = jnp.sum(jnp.where(taken, values, 0), axis=1, keepdims=True, dtype=jnp.int32)
        table = jnp.where(list_lane == which, listed, table)
    lists[...] = table
    load_lists = pltpu.make_async_copy(lists, index_ref, load_sem.at[3])
    load_lists.start()

    load_b.wait()
    pl.semaphore_wait(barrier, n_row + n_col - 2)

    def line_copy(way, step, slot_chip, to_chip):
        held = pl.ds((slot_chip * 2 + core) * held_blocks, held_blocks)
        return pltpu.make_async_remote_copy(
            src_ref=b_all.at[held],
            dst_ref=b_all.at[held],
            send_sem=line_send.at[way, step],
            recv_sem=line_recv.at[way, step],
            device_id=(to_chip * 2 + core, col),
            device_id_type=MESH,
        )

    def pair_copy(number, slot_row):
        held = pl.ds(slot_row * held_blocks, held_blocks)
        return pltpu.make_async_remote_copy(
            src_ref=b_all.at[held],
            dst_ref=b_all.at[held],
            send_sem=pair_send.at[number],
            recv_sem=pair_recv.at[number],
            device_id=(other, col),
            device_id_type=MESH,
        )

    def has(way, step):
        return chip >= 1 + step if way == 0 else chip + 1 + step < chips

    def sends(way, step):
        if way == 0:
            return (chip < chips - 1) & (chip >= step)
        return (chip > 0) & (chip + step < chips)

    def sent_chip(way, step):
        return chip - step if way == 0 else chip + step

    def next_chip(way):
        return chip + 1 if way == 0 else chip - 1

    for way in range(2):

        @pl.when(sends(way, 0))
        def _():
            line_copy(way, 0, sent_chip(way, 0), next_chip(way)).start()

    pair_copy(0, row).start()

    load_c.wait()
    third = c_ref[...]
    high, low = split(third)
    c_high[...] = high.reshape(c_high.shape)
    c_low[...] = low.reshape(c_low.shape)
    gram3[...] = jnp.zeros_like(gram3)
    mixed[...] = jnp.zeros_like(mixed)
    add_squares(gram3, mixed, third)
    gram3[...] += mixed[...] + mixed[...].T
    gram2[...] = jnp.zeros_like(gram2)
    mixed[...] = jnp.zeros_like(mixed)
    load_x.wait()
    load_lists.wait()
    lane = lax.broadcasted_iota(jnp.int32, (edge, 128), 1)
    lane_row = lax.broadcasted_iota(jnp.int32, (1, 128), 1) // edge
    one_mask = [jnp.where(lane_row == m, 1.0, 0.0).astype(jnp.bfloat16) for m in range(4)]
    two_mask = [jnp.where(lane_row % 2 == m, 1.0, 0.0).astype(jnp.bfloat16) for m in range(2)]
    chunks = edge * edge // 128

    def tile(slot, second):
        third_at = index_ref[slot, 2]
        tile_at = index_ref[slot, 0]
        weights = jnp.concatenate([c_high[third_at]] * 6 + [c_low[third_at]] * 2, axis=0)
        pieces = []
        for q in range(chunks):
            x = x_ref[tile_at, :, q * 128 : (q + 1) * 128]
            first = x.astype(jnp.bfloat16)
            x_high = first.astype(jnp.float32)
            x_low = x - x_high
            turned_high = pltpu.roll(x_high, 64, 1)
            turned_low = pltpu.roll(x_low, 64, 1)
            front = jnp.where(lane < 64, x_low, turned_high).astype(jnp.bfloat16)
            back = jnp.where(lane < 64, turned_low, x_high).astype(jnp.bfloat16)
            for m in range(4):
                rest = front if m < 2 else back
                pieces.append(
                    jnp.concatenate([first * one_mask[m], rest * two_mask[m % 2]], axis=1)
                )
        inner = jnp.dot(
            jnp.concatenate(pieces, axis=0), weights, preferred_element_type=jnp.float32
        )
        total = inner[:edge] * second[0:1]
        for j in range(1, edge):
            total = total + inner[j * edge : (j + 1) * edge] * second[j : j + 1]
        partials[:, pl.ds(slot, 1), :] = total[:, None, :]

    def use(held_chip):
        for side in range(2):
            held = b_all[pl.ds((held_chip * 2 + side) * held_blocks, held_blocks)]
            b_now[side] = held
            flat = held.reshape(held_blocks * edge, rank)
            add_squares(gram2, mixed, flat)

    def tiles_of(held_chip):
        def pair(s, carried):
            for side in range(2):
                slot = (held_chip * 2 + side) * per_row + s
                tile(slot, b_now[side, index_ref[slot, 1]])
            return carried

        lax.fori_loop(0, per_row, pair, 0)

    def gram_copy(step, which):
        to_col = (col + step) % n_col
        source = gram2 if which == 0 else gram3
        return pltpu.make_async_remote_copy(
            src_ref=source.at[pl.ds(pl.multiple_of(row * piece, 8), piece)],
            dst_ref=gram_in.at[which, step],
            send_sem=gram_send.at[which, step],
            recv_sem=gram_recv.at[which, step],
            device_id=(row, to_col),
            device_id_type=MESH,
        )

    nearer = jnp.minimum(chip, chips - 1 - chip)

    def turn(number, carried):
        step = number - 1
        for way in range(2):

            @pl.when((number > 0) & has(way, step))
            def _():
                held = sent_chip(way, step + 1)
                line_copy(way, step, held, next_chip(way)).wait_recv()

                @pl.when((step + 1 < chips - 1) & sends(way, step + 1))
                def _():
                    line_copy(way, step + 1, held, next_chip(way)).start()

                pair_copy(1 + 2 * step + way, held * 2 + core).start()

        both = jnp.where(number % 2 == 1, chip - (number + 1) // 2, chip + number // 2)
        one = jnp.where(
            chip < chips - 1 - chip, chip + number - nearer, chip - number + nearer
        )
        held = jnp.where(number <= 2 * nearer, both, one)
        pair_at = jnp.where(held < chip, 2 * (chip - held) - 1, 2 * (held - chip))
        pair_copy(pair_at, held * 2 + 1 - core).wait_recv()
        use(held)

        @pl.when(number == chips - 1)
        def _():
            gram2[...] += mixed[...] + mixed[...].T
            for to_step in range(1, n_col):
                gram_copy(to_step, 0).start()
                gram_copy(to_step, 1).start()

        tiles_of(held)
        return carried

    lax.fori_loop(0, chips, turn, 0)

    for step in range(1, n_col):
        gram_copy(step, 0).wait_recv()
        gram_copy(step, 1).wait_recv()
    own_piece = pl.ds(pl.multiple_of(row * piece, 8), piece)
    sum2, sum3 = gram2[own_piece, :], gram3[own_piece, :]
    for step in range(1, n_col):
        sum2 = sum2 + gram_in[0, step]
        sum3 = sum3 + gram_in[1, step]
    normal_in[row] = sum2 * sum3

    def normal_copy(step, slot):
        return pltpu.make_async_remote_copy(
            src_ref=normal_in.at[slot],
            dst_ref=normal_in.at[slot],
            send_sem=normal_send.at[step],
            recv_sem=normal_recv.at[step],
            device_id=((row + step) % n_row, col),
            device_id_type=MESH,
        )

    for step in range(1, n_row):
        normal_copy(step, row).start()

    targets = n_col * IB_DEV
    code_line = lists[:, 3:4]
    same = lax.broadcasted_iota(jnp.int32, (slots, slots), 0) == lax.broadcasted_iota(
        jnp.int32, (slots, slots), 1
    )
    code_lane = jnp.sum(jnp.where(same, code_line, 0), axis=0, keepdims=True, dtype=jnp.int32)
    chosen = lax.broadcasted_iota(jnp.int32, (targets, slots), 0) + 1 == code_lane
    chosen = jnp.where(chosen, 1.0, 0.0)
    chosen = jnp.concatenate([chosen, chosen], axis=1).astype(jnp.bfloat16)

    live = code_line > 0

    def choose(group, carried):
        for part in range(4):
            i = group * 4 + part
            high, low = split(jnp.where(live, partials[i], 0.0))
            rows = jnp.dot(
                chosen, jnp.concatenate([high, low], axis=0), preferred_element_type=jnp.float32
            )
            for c in range(n_col):
                send[c, pl.ds(pl.multiple_of(i * IB_DEV, IB_DEV), IB_DEV), :] = rows[
                    c * IB_DEV : (c + 1) * IB_DEV
                ]
        return carried

    lax.fori_loop(0, edge // 4, choose, 0)

    def block_copy(number, source, target, to_col):
        return pltpu.make_async_remote_copy(
            src_ref=source,
            dst_ref=target,
            send_sem=block_send.at[number],
            recv_sem=block_recv.at[number],
            device_id=(row, to_col),
            device_id_type=MESH,
        )

    half = rows_out // 2
    halves = (pl.ds(0, half), pl.ds(half, half))
    copies = []
    later = []
    if n_col == 4:
        near = (col // 2) * 2 + 1 - col % 2
        far = (1 - col // 2) * 2 + col % 2
        corner = (1 - col // 2) * 2 + 1 - col % 2
        sides = (near, far)
        for way in range(2):
            copies.append(
                block_copy(way, send.at[corner, halves[way]], arrive.at[0, halves[way]], sides[way])
            )
        for way in range(2):
            copies.append(
                block_copy(2 + way, send.at[sides[way], halves[way]], arrive.at[1, halves[way]], sides[way])
            )
        for way in range(2):
            later.append(
                block_copy(4 + way, send.at[sides[1 - way], halves[way]], arrive.at[2, halves[way]], sides[1 - way])
            )
    else:
        for step in range(1, n_col):
            to_col = (col + step) % n_col
            copies.append(block_copy(step - 1, send.at[to_col], arrive.at[step - 1], to_col))
    for copy in copies:
        copy.start()

    for step in range(1, n_row):
        normal_copy(step, (row + n_row - step) % n_row).wait_recv()
    matrix = jnp.concatenate([normal_in[r] for r in range(n_row)], axis=0)
    pivots = rank // PIVOT
    rows = matrix[:PIVOT]
    early = 3 * pivots // 8
    for at in range(early):
        matrix, rows = eliminate(matrix, rows, at)
    if later:
        for way in range(2):
            copies[way].wait_recv()
            send[sides[1 - way], halves[way]] += arrive[0, halves[way]]
            later[way].start()
    for at in range(early, pivots):
        matrix, rows = eliminate(matrix, rows, at)

    total = send[col]
    if later:
        for copy in copies[2:] + later:
            copy.wait_recv()
        total = total + arrive[1] + arrive[2]
    else:
        for copy in copies:
            copy.wait_recv()
        for step in range(n_col - 1):
            total = total + arrive[step]
    solved = exact_dot(total, matrix)
    for i in range(edge):
        out_ref[:, i : i + 1, :] = solved[i * IB_DEV : (i + 1) * IB_DEV][:, None, :]

    for copy in copies + later:
        copy.wait_send()
    for step in range(1, n_row):
        normal_copy(step, row).wait_send()
    for step in range(1, n_col):
        gram_copy(step, 0).wait_send()
        gram_copy(step, 1).wait_send()
    pair_copy(0, row).wait_send()
    for step in range(chips - 1):
        for way in range(2):

            @pl.when(has(way, step))
            def _():
                pair_copy(1 + 2 * step + way, sent_chip(way, step + 1) * 2 + core).wait_send()

            @pl.when(sends(way, step))
            def _():
                line_copy(way, step, sent_chip(way, step), next_chip(way)).wait_send()


def local(
    n_row,
    n_col,
    tile_values,
    tile_count,
    mode1_column,
    mode1_offset,
    mode2_row,
    mode2_offset,
    mode3_offset,
    mode2_factor,
    mode3_factor,
):
    slots, edge = tile_values.shape[0], tile_values.shape[1]
    rows_held, rank = mode2_factor.shape
    blocks_held = rows_held // edge
    row_most = {8: 7, 16: 4}.get(n_row, slots)
    places = n_row * row_most
    lists = jnp.stack(
        [mode2_row[:, 0], mode2_offset, mode3_offset, mode1_column[:, 0], mode1_offset]
    )
    rows_out = IB_DEV * edge
    piece = rank // n_row
    chips = n_row // 2
    f32, bf16 = jnp.float32, jnp.bfloat16
    dma = pltpu.SemaphoreType.DMA
    vmem = pl.BlockSpec(memory_space=pltpu.VMEM)
    smem = pl.BlockSpec(memory_space=pltpu.SMEM)
    hbm = pl.BlockSpec(memory_space=pltpu.HBM)
    blocks = max(6, n_col - 1)
    out = pl.pallas_call(
        functools.partial(kernel, n_row, n_col, row_most),
        out_shape=jax.ShapeDtypeStruct((IB_DEV, edge, rank), f32),
        in_specs=[smem, vmem, hbm, hbm, hbm],
        out_specs=vmem,
        scratch_shapes=[
            pltpu.VMEM((places, 128), jnp.int32),
            pltpu.SMEM((places, 128), jnp.int32),
            pltpu.VMEM(tile_values.shape, f32),
            pltpu.VMEM((n_row * blocks_held, edge, rank), f32),
            pltpu.VMEM((2, blocks_held, edge, rank), f32),
            pltpu.VMEM(mode3_factor.shape, f32),
            pltpu.VMEM((mode3_factor.shape[0] // edge, edge, rank), bf16),
            pltpu.VMEM((mode3_factor.shape[0] // edge, edge, rank), bf16),
            pltpu.VMEM((rank, rank), f32),
            pltpu.VMEM((rank, rank), f32),
            pltpu.VMEM((rank, rank), f32),
            pltpu.VMEM((2, n_col, piece, rank), f32),
            pltpu.VMEM((n_row, piece, rank), f32),
            pltpu.VMEM((edge, places, rank), f32),
            pltpu.VMEM((n_col, rows_out, rank), f32),
            pltpu.VMEM((max(3, n_col - 1), rows_out, rank), f32),
            dma((4,)),
            dma((2, chips)),
            dma((2, chips)),
            dma((2 * chips,)),
            dma((2 * chips,)),
            dma((2, n_col)),
            dma((2, n_col)),
            dma((n_row,)),
            dma((n_row,)),
            dma((blocks,)),
            dma((blocks,)),
        ],
        compiler_params=pltpu.CompilerParams(
            collective_id=0, has_side_effects=True, vmem_limit_bytes=60 * 2**20
        ),
    )(tile_count, lists, tile_values, mode2_factor.reshape(blocks_held, edge, rank), mode3_factor)
    return out.reshape(rows_out, rank)


def solution(mesh):
    placed = (
        P(("row", "col"), None, None),
        P(("row", "col")),
        P(("row", "col"), None),
        P(("row", "col")),
        P(("row", "col"), None),
        P(("row", "col")),
        P(("row", "col")),
        P(("row", "col"), None),
        P("col", None),
    )
    return jax.shard_map(
        functools.partial(local, mesh.shape["row"], mesh.shape["col"]),
        mesh=mesh,
        in_specs=placed,
        out_specs=P(("row", "col"), None),
        check_vma=False,
    )
```

```python
import functools

import jax
import jax.numpy as jnp
from jax import lax
from jax.experimental import pallas as pl
from jax.experimental.pallas import tpu as pltpu
from jax.sharding import PartitionSpec as P

IB_DEV = 16
PIVOT = 32
SPREAD = 8
PIECES = 4
MESH = pl.DeviceIdType.MESH
HIGHEST = lax.Precision.HIGHEST


def exact_dot(left, right, contract=((1,), (0,))):
    return lax.dot_general(
        left, right, (contract, ((), ())), precision=HIGHEST, preferred_element_type=jnp.float32
    )


def split(values):
    high = values.astype(jnp.bfloat16)
    return high, (values - high.astype(jnp.float32)).astype(jnp.bfloat16)


def split_three(values):
    high = values.astype(jnp.bfloat16)
    rest = values - high.astype(jnp.float32)
    middle = rest.astype(jnp.bfloat16)
    return high, middle, (rest - middle.astype(jnp.float32)).astype(jnp.bfloat16)


def invert_small(block):
    size = block.shape[0]
    line = lax.broadcasted_iota(jnp.int32, (size, size), 0)
    lane = lax.broadcasted_iota(jnp.int32, (size, size), 1)
    lane_row = lax.broadcasted_iota(jnp.int32, (1, size), 1)
    for first in range(0, size, SPREAD):
        columns = [
            jnp.broadcast_to(block[:, k : k + 1], (size, size))
            for k in range(first, first + SPREAD)
        ]
        for k in range(first, first + SPREAD):
            column = columns[k - first]
            scale = 1.0 / column[k : k + 1, :]
            row = jnp.where(lane_row == k, scale, block[k : k + 1, :] * scale)
            kept = jnp.where(lane == k, 0.0, block)
            block = jnp.where(line == k, row, kept - column * row)
            for later in range(k + 1 - first, SPREAD):
                entry = columns[later][k : k + 1, :] * scale
                columns[later] = jnp.where(line == k, entry, columns[later] - column * entry)
    return block


def eliminate(matrix, rows, at):
    size = matrix.shape[0]
    start = at * PIVOT
    lane = lax.broadcasted_iota(jnp.int32, (PIVOT, size), 1)
    line = lax.broadcasted_iota(jnp.int32, (PIVOT, size), 0)
    inside = (lane >= start) & (lane < start + PIVOT)
    pivot = invert_small(rows[:, start : start + PIVOT])
    unit = jnp.where(lane - start == line, 1.0, 0.0)
    high, middle, low = split_three(jnp.where(inside, unit, rows))
    p_high, p_middle, p_low = split_three(pivot)
    new_rows = jnp.dot(
        jnp.concatenate([p_high, p_high, p_middle, p_high, p_middle, p_low], axis=1),
        jnp.concatenate([high, middle, high, low, middle, high], axis=0),
        preferred_element_type=jnp.float32,
    )
    c_high, c_middle, c_low = split_three(jnp.where(lane < start, -rows, rows))
    high, middle, low = split_three(new_rows)
    left = jnp.concatenate([c_high, c_high, c_middle, c_high, c_middle, c_low], axis=0)
    right = jnp.concatenate([high, middle, high, low, middle, high], axis=0)

    def change(part):
        return lax.dot_general(
            part, right, (((0,), (0,)), ((), ())), preferred_element_type=jnp.float32
        )

    after = start + PIVOT
    next_rows = None
    if after < size:
        next_rows = jnp.where(inside, 0.0, matrix[after : after + PIVOT]) - change(
            left[:, after : after + PIVOT]
        )
    lane_all = lax.broadcasted_iota(jnp.int32, (size, size), 1)
    inside_all = (lane_all >= start) & (lane_all < after)
    rest = jnp.where(inside_all, 0.0, matrix) - change(left)
    pieces = [rest[:start], new_rows, rest[after:]]
    matrix = jnp.concatenate([piece for piece in pieces if piece.shape[0]], axis=0)
    return matrix, next_rows


def add_squares(squares, mixed, values):
    high, middle = split(values)
    contract = (((0,), (0,)), ((), ()))
    both = lax.dot_general(
        high, jnp.concatenate([high, middle], axis=1), contract, preferred_element_type=jnp.float32
    )
    rest = lax.dot_general(middle, middle, contract, preferred_element_type=jnp.float32)
    width = values.shape[1]
    squares[...] += both[:, :width] + rest
    mixed[...] += both[:, width:]


def kernel(
    n_row,
    n_col,
    row_most,
    count_ref,
    owner_ref,
    second_ref,
    third_ref,
    target_col_ref,
    target_ref,
    x_hbm,
    b_hbm,
    c_hbm,
    out_ref,
    lists,
    index_ref,
    x_ref,
    b_all,
    b_now,
    c_ref,
    c_high,
    c_low,
    gram2,
    gram3,
    mixed,
    gram_in,
    normal_in,
    partials,
    send,
    arrive,
    load_sem,
    line_send,
    line_recv,
    pair_send,
    pair_recv,
    gram_send,
    gram_recv,
    normal_send,
    normal_recv,
    block_send,
    block_recv,
):
    row = lax.axis_index("row")
    col = lax.axis_index("col")
    chip, core = row // 2, row % 2
    chips = n_row // 2
    other = chip * 2 + 1 - core
    edge = x_ref.shape[1]
    slots = lists.shape[0]
    per_row = row_most
    rank = c_ref.shape[1]
    piece = rank // n_row
    rows_out = IB_DEV * edge
    held_blocks = b_hbm.shape[0]
    own_blocks = pl.ds(row * held_blocks, held_blocks)

    load_b = pltpu.make_async_copy(b_hbm, b_all.at[own_blocks], load_sem.at[0])
    load_c = pltpu.make_async_copy(c_hbm, c_ref, load_sem.at[1])
    load_x = pltpu.make_async_copy(x_hbm, x_ref, load_sem.at[2])
    load_b.start()
    load_c.start()
    load_x.start()

    barrier = pltpu.get_barrier_semaphore()
    for step in range(1, n_row):
        pl.semaphore_signal(
            barrier, inc=1, device_id=((row + step) % n_row, col), device_id_type=MESH
        )
    for step in range(1, n_col):
        pl.semaphore_signal(
            barrier, inc=1, device_id=(row, (col + step) % n_col), device_id_type=MESH
        )
    tiles = owner_ref.shape[1]
    tile_line = lax.broadcasted_iota(jnp.int32, (tiles, tiles), 0)
    tile_lane = lax.broadcasted_iota(jnp.int32, (tiles, tiles), 1)
    owner = owner_ref[...]
    owner_line = jnp.sum(
        jnp.where(tile_line == tile_lane, owner, 0), axis=1, keepdims=True, dtype=jnp.int32
    )
    before = (owner_line == owner) & (tile_line < tile_lane)
    place = owner * row_most + jnp.sum(
        jnp.where(before, 1, 0), axis=0, keepdims=True, dtype=jnp.int32
    )
    taken = lax.broadcasted_iota(jnp.int32, (slots, tiles), 0) == place
    number = lax.broadcasted_iota(jnp.int32, (1, tiles), 1)
    code = jnp.where(number < count_ref[0], target_col_ref[...] * IB_DEV + target_ref[...] + 1, 0)
    list_lane = lax.broadcasted_iota(jnp.int32, lists.shape, 1)
    table = jnp.zeros(lists.shape, jnp.int32)
    for which, values in enumerate((number, second_ref[...], third_ref[...], code)):
        listed = jnp.sum(jnp.where(taken, values, 0), axis=1, keepdims=True, dtype=jnp.int32)
        table = jnp.where(list_lane == which, listed, table)
    lists[...] = table
    load_lists = pltpu.make_async_copy(lists, index_ref, load_sem.at[3])
    load_lists.start()

    load_b.wait()
    pl.semaphore_wait(barrier, n_row + n_col - 2)

    def line_copy(way, step, slot_chip, to_chip):
        held = pl.ds((slot_chip * 2 + core) * held_blocks, held_blocks)
        return pltpu.make_async_remote_copy(
            src_ref=b_all.at[held],
            dst_ref=b_all.at[held],
            send_sem=line_send.at[way, step],
            recv_sem=line_recv.at[way, step],
            device_id=(to_chip * 2 + core, col),
            device_id_type=MESH,
        )

    def pair_copy(number, slot_row):
        held = pl.ds(slot_row * held_blocks, held_blocks)
        return pltpu.make_async_remote_copy(
            src_ref=b_all.at[held],
            dst_ref=b_all.at[held],
            send_sem=pair_send.at[number],
            recv_sem=pair_recv.at[number],
            device_id=(other, col),
            device_id_type=MESH,
        )

    def has(way, step):
        return chip >= 1 + step if way == 0 else chip + 1 + step < chips

    def sends(way, step):
        if way == 0:
            return (chip < chips - 1) & (chip >= step)
        return (chip > 0) & (chip + step < chips)

    def sent_chip(way, step):
        return chip - step if way == 0 else chip + step

    def next_chip(way):
        return chip + 1 if way == 0 else chip - 1

    for way in range(2):

        @pl.when(sends(way, 0))
        def _():
            line_copy(way, 0, sent_chip(way, 0), next_chip(way)).start()

    pair_copy(0, row).start()

    load_c.wait()
    third = c_ref[...]
    high, low = split(third)
    c_high[...] = high.reshape(c_high.shape)
    c_low[...] = low.reshape(c_low.shape)
    gram3[...] = jnp.zeros_like(gram3)
    mixed[...] = jnp.zeros_like(mixed)
    add_squares(gram3, mixed, third)
    gram3[...] += mixed[...] + mixed[...].T
    gram2[...] = jnp.zeros_like(gram2)
    mixed[...] = jnp.zeros_like(mixed)
    load_x.wait()
    load_lists.wait()
    lane = lax.broadcasted_iota(jnp.int32, (edge, 128), 1)
    lane_row = lax.broadcasted_iota(jnp.int32, (1, 128), 1) // edge
    one_mask = [jnp.where(lane_row == m, 1.0, 0.0).astype(jnp.bfloat16) for m in range(4)]
    two_mask = [jnp.where(lane_row % 2 == m, 1.0, 0.0).astype(jnp.bfloat16) for m in range(2)]
    chunks = edge * edge // 128

    def tile(slot, second):
        third_at = index_ref[slot, 2]
        tile_at = index_ref[slot, 0]
        weights = jnp.concatenate([c_high[third_at]] * 6 + [c_low[third_at]] * 2, axis=0)
        pieces = []
        for q in range(chunks):
            x = x_ref[tile_at, :, q * 128 : (q + 1) * 128]
            first = x.astype(jnp.bfloat16)
            x_high = first.astype(jnp.float32)
            x_low = x - x_high
            turned_high = pltpu.roll(x_high, 64, 1)
            turned_low = pltpu.roll(x_low, 64, 1)
            front = jnp.where(lane < 64, x_low, turned_high).astype(jnp.bfloat16)
            back = jnp.where(lane < 64, turned_low, x_high).astype(jnp.bfloat16)
            for m in range(4):
                rest = front if m < 2 else back
                pieces.append(
                    jnp.concatenate([first * one_mask[m], rest * two_mask[m % 2]], axis=1)
                )
        inner = jnp.dot(
            jnp.concatenate(pieces, axis=0), weights, preferred_element_type=jnp.float32
        )
        total = inner[:edge] * second[0:1]
        for j in range(1, edge):
            total = total + inner[j * edge : (j + 1) * edge] * second[j : j + 1]
        partials[:, pl.ds(slot, 1), :] = total[:, None, :]

    def use(held_chip):
        for side in range(2):
            held = b_all[pl.ds((held_chip * 2 + side) * held_blocks, held_blocks)]
            b_now[side] = held
            flat = held.reshape(held_blocks * edge, rank)
            add_squares(gram2, mixed, flat)

    def tiles_of(held_chip):
        def pair(s, carried):
            for side in range(2):
                slot = (held_chip * 2 + side) * per_row + s
                tile(slot, b_now[side, index_ref[slot, 1]])
            return carried

        lax.fori_loop(0, per_row, pair, 0)

    def gram_copy(step, which):
        to_col = (col + step) % n_col
        source = gram2 if which == 0 else gram3
        return pltpu.make_async_remote_copy(
            src_ref=source.at[pl.ds(pl.multiple_of(row * piece, 8), piece)],
            dst_ref=gram_in.at[which, step],
            send_sem=gram_send.at[which, step],
            recv_sem=gram_recv.at[which, step],
            device_id=(row, to_col),
            device_id_type=MESH,
        )

    nearer = jnp.minimum(chip, chips - 1 - chip)

    def turn(number, carried):
        step = number - 1
        for way in range(2):

            @pl.when((number > 0) & has(way, step))
            def _():
                held = sent_chip(way, step + 1)
                line_copy(way, step, held, next_chip(way)).wait_recv()

                @pl.when((step + 1 < chips - 1) & sends(way, step + 1))
                def _():
                    line_copy(way, step + 1, held, next_chip(way)).start()

                pair_copy(1 + 2 * step + way, held * 2 + core).start()

        both = jnp.where(number % 2 == 1, chip - (number + 1) // 2, chip + number // 2)
        one = jnp.where(
            chip < chips - 1 - chip, chip + number - nearer, chip - number + nearer
        )
        held = jnp.where(number <= 2 * nearer, both, one)
        pair_at = jnp.where(held < chip, 2 * (chip - held) - 1, 2 * (held - chip))
        pair_copy(pair_at, held * 2 + 1 - core).wait_recv()
        use(held)

        @pl.when(number == chips - 1)
        def _():
            gram2[...] += mixed[...] + mixed[...].T
            for to_step in range(1, n_col):
                gram_copy(to_step, 0).start()
                gram_copy(to_step, 1).start()

        tiles_of(held)
        return carried

    lax.fori_loop(0, chips, turn, 0)

    for step in range(1, n_col):
        gram_copy(step, 0).wait_recv()
        gram_copy(step, 1).wait_recv()
    own_piece = pl.ds(pl.multiple_of(row * piece, 8), piece)
    sum2, sum3 = gram2[own_piece, :], gram3[own_piece, :]
    for step in range(1, n_col):
        sum2 = sum2 + gram_in[0, step]
        sum3 = sum3 + gram_in[1, step]
    normal_in[row] = sum2 * sum3

    def normal_copy(step, slot):
        return pltpu.make_async_remote_copy(
            src_ref=normal_in.at[slot],
            dst_ref=normal_in.at[slot],
            send_sem=normal_send.at[step],
            recv_sem=normal_recv.at[step],
            device_id=((row + step) % n_row, col),
            device_id_type=MESH,
        )

    for step in range(1, n_row):
        normal_copy(step, row).start()

    targets = n_col * IB_DEV
    code_line = lists[:, 3:4]
    same = lax.broadcasted_iota(jnp.int32, (slots, slots), 0) == lax.broadcasted_iota(
        jnp.int32, (slots, slots), 1
    )
    code_lane = jnp.sum(jnp.where(same, code_line, 0), axis=0, keepdims=True, dtype=jnp.int32)
    chosen = lax.broadcasted_iota(jnp.int32, (targets, slots), 0) + 1 == code_lane
    chosen = jnp.where(chosen, 1.0, 0.0)
    chosen = jnp.concatenate([chosen, chosen], axis=1).astype(jnp.bfloat16)

    live = code_line > 0

    def block_copy(number, source, target, to_col):
        return pltpu.make_async_remote_copy(
            src_ref=source,
            dst_ref=target,
            send_sem=block_send.at[number],
            recv_sem=block_recv.at[number],
            device_id=(row, to_col),
            device_id_type=MESH,
        )

    def choose(group, carried):
        for part in range(4):
            i = group * 4 + part
            high, low = split(jnp.where(live, partials[i], 0.0))
            rows = jnp.dot(
                chosen, jnp.concatenate([high, low], axis=0), preferred_element_type=jnp.float32
            )
            for c in range(n_col):
                send[c, pl.ds(pl.multiple_of(i * IB_DEV, IB_DEV), IB_DEV), :] = rows[
                    c * IB_DEV : (c + 1) * IB_DEV
                ]
        return carried

    lines = edge // PIECES
    length = lines * IB_DEV
    pieces = [pl.ds(number * length, length) for number in range(PIECES)]
    corners, beside, later = [], [], []
    if n_col == 4:
        near = (col // 2) * 2 + 1 - col % 2
        far = (1 - col // 2) * 2 + col % 2
        corner = (1 - col // 2) * 2 + 1 - col % 2
        sides = (near, far)
        for number, held in enumerate(pieces):
            first, second = sides[number % 2], sides[1 - number % 2]
            corners.append(block_copy(number, send.at[corner, held], arrive.at[0, held], first))
            beside.append(
                block_copy(PIECES + number, send.at[first, held], arrive.at[1, held], first)
            )
            later.append(
                block_copy(2 * PIECES + number, send.at[second, held], arrive.at[2, held], second)
            )
    else:
        for step in range(1, n_col):
            to_col = (col + step) % n_col
            beside.append(block_copy(step - 1, send.at[to_col], arrive.at[step - 1], to_col))
    for number in range(PIECES):
        lax.fori_loop(number * lines // 4, (number + 1) * lines // 4, choose, 0)
        if corners:
            corners[number].start()
    for copy in beside:
        copy.start()

    for step in range(1, n_row):
        normal_copy(step, (row + n_row - step) % n_row).wait_recv()
    matrix = jnp.concatenate([normal_in[r] for r in range(n_row)], axis=0)
    pivots = rank // PIVOT
    rows = matrix[:PIVOT]
    for at in range(pivots):
        matrix, rows = eliminate(matrix, rows, at)
        for number in range(len(later)):
            if at == (1 + 2 * (number // 2)) * pivots // 8:
                held, second = pieces[number], sides[1 - number % 2]
                corners[number].wait_recv()
                send[second, held] += arrive[0, held]
                later[number].start()

    if not later:
        for copy in beside:
            copy.wait_recv()
    for number, held in enumerate(pieces):
        total = send[col, held]
        if later:
            beside[number].wait_recv()
            later[number].wait_recv()
            total = total + arrive[1, held] + arrive[2, held]
        else:
            for step in range(n_col - 1):
                total = total + arrive[step, held]
        solved = exact_dot(total, matrix)
        for i in range(lines):
            out_ref[:, pl.ds(number * lines + i, 1), :] = solved[
                i * IB_DEV : (i + 1) * IB_DEV
            ][:, None, :]

    for copy in corners + beside + later:
        copy.wait_send()
    for step in range(1, n_row):
        normal_copy(step, row).wait_send()
    for step in range(1, n_col):
        gram_copy(step, 0).wait_send()
        gram_copy(step, 1).wait_send()
    pair_copy(0, row).wait_send()
    for step in range(chips - 1):
        for way in range(2):

            @pl.when(has(way, step))
            def _():
                pair_copy(1 + 2 * step + way, sent_chip(way, step + 1) * 2 + core).wait_send()

            @pl.when(sends(way, step))
            def _():
                line_copy(way, step, sent_chip(way, step), next_chip(way)).wait_send()


def local(
    n_row,
    n_col,
    tile_values,
    tile_count,
    mode1_column,
    mode1_offset,
    mode2_row,
    mode2_offset,
    mode3_offset,
    mode2_factor,
    mode3_factor,
):
    slots, edge = tile_values.shape[0], tile_values.shape[1]
    rows_held, rank = mode2_factor.shape
    blocks_held = rows_held // edge
    row_most = {8: 7, 16: 4}.get(n_row, slots)
    places = n_row * row_most
    lists = [
        values.reshape(1, slots)
        for values in (mode2_row, mode2_offset, mode3_offset, mode1_column, mode1_offset)
    ]
    rows_out = IB_DEV * edge
    piece = rank // n_row
    chips = n_row // 2
    f32, bf16 = jnp.float32, jnp.bfloat16
    dma = pltpu.SemaphoreType.DMA
    vmem = pl.BlockSpec(memory_space=pltpu.VMEM)
    smem = pl.BlockSpec(memory_space=pltpu.SMEM)
    hbm = pl.BlockSpec(memory_space=pltpu.HBM)
    blocks = max(3 * PIECES, n_col - 1)
    out = pl.pallas_call(
        functools.partial(kernel, n_row, n_col, row_most),
        out_shape=jax.ShapeDtypeStruct((IB_DEV, edge, rank), f32),
        in_specs=[smem] + [vmem] * 5 + [hbm, hbm, hbm],
        out_specs=vmem,
        scratch_shapes=[
            pltpu.VMEM((places, 128), jnp.int32),
            pltpu.SMEM((places, 128), jnp.int32),
            pltpu.VMEM(tile_values.shape, f32),
            pltpu.VMEM((n_row * blocks_held, edge, rank), f32),
            pltpu.VMEM((2, blocks_held, edge, rank), f32),
            pltpu.VMEM(mode3_factor.shape, f32),
            pltpu.VMEM((mode3_factor.shape[0] // edge, edge, rank), bf16),
            pltpu.VMEM((mode3_factor.shape[0] // edge, edge, rank), bf16),
            pltpu.VMEM((rank, rank), f32),
            pltpu.VMEM((rank, rank), f32),
            pltpu.VMEM((rank, rank), f32),
            pltpu.VMEM((2, n_col, piece, rank), f32),
            pltpu.VMEM((n_row, piece, rank), f32),
            pltpu.VMEM((edge, places, rank), f32),
            pltpu.VMEM((n_col, rows_out, rank), f32),
            pltpu.VMEM((max(3, n_col - 1), rows_out, rank), f32),
            dma((4,)),
            dma((2, chips)),
            dma((2, chips)),
            dma((2 * chips,)),
            dma((2 * chips,)),
            dma((2, n_col)),
            dma((2, n_col)),
            dma((n_row,)),
            dma((n_row,)),
            dma((blocks,)),
            dma((blocks,)),
        ],
        compiler_params=pltpu.CompilerParams(
            collective_id=0, has_side_effects=True, vmem_limit_bytes=60 * 2**20
        ),
    )(tile_count, *lists, tile_values, mode2_factor.reshape(blocks_held, edge, rank), mode3_factor)
    return out.reshape(rows_out, rank)


def solution(mesh):
    placed = (
        P(("row", "col"), None, None),
        P(("row", "col")),
        P(("row", "col"), None),
        P(("row", "col")),
        P(("row", "col"), None),
        P(("row", "col")),
        P(("row", "col")),
        P(("row", "col"), None),
        P("col", None),
    )
    return jax.shard_map(
        functools.partial(local, mesh.shape["row"], mesh.shape["col"]),
        mesh=mesh,
        in_specs=placed,
        out_specs=P(("row", "col"), None),
        check_vma=False,
    )
```

```python
import functools

import jax
import jax.numpy as jnp
from jax import lax
from jax.experimental import pallas as pl
from jax.experimental.pallas import tpu as pltpu
from jax.sharding import PartitionSpec as P

IB_DEV = 16
PIVOT = 32
SPREAD = 8
PIECES = 4
MESH = pl.DeviceIdType.MESH
HIGHEST = lax.Precision.HIGHEST


def exact_dot(left, right, contract=((1,), (0,))):
    return lax.dot_general(
        left, right, (contract, ((), ())), precision=HIGHEST, preferred_element_type=jnp.float32
    )


def split(values):
    high = values.astype(jnp.bfloat16)
    return high, (values - high.astype(jnp.float32)).astype(jnp.bfloat16)


def split_three(values):
    high = values.astype(jnp.bfloat16)
    rest = values - high.astype(jnp.float32)
    middle = rest.astype(jnp.bfloat16)
    return high, middle, (rest - middle.astype(jnp.float32)).astype(jnp.bfloat16)


def invert_small(block):
    size = block.shape[0]
    line = lax.broadcasted_iota(jnp.int32, (size, size), 0)
    lane = lax.broadcasted_iota(jnp.int32, (size, size), 1)
    lane_row = lax.broadcasted_iota(jnp.int32, (1, size), 1)
    for first in range(0, size, SPREAD):
        columns = [
            jnp.broadcast_to(block[:, k : k + 1], (size, size))
            for k in range(first, first + SPREAD)
        ]
        for k in range(first, first + SPREAD):
            column = columns[k - first]
            scale = 1.0 / column[k : k + 1, :]
            row = jnp.where(lane_row == k, scale, block[k : k + 1, :] * scale)
            kept = jnp.where(lane == k, 0.0, block)
            block = jnp.where(line == k, row, kept - column * row)
            for later in range(k + 1 - first, SPREAD):
                entry = columns[later][k : k + 1, :] * scale
                columns[later] = jnp.where(line == k, entry, columns[later] - column * entry)
    return block


def eliminate(matrix, rows, at):
    size = matrix.shape[0]
    start = at * PIVOT
    lane = lax.broadcasted_iota(jnp.int32, (PIVOT, size), 1)
    line = lax.broadcasted_iota(jnp.int32, (PIVOT, size), 0)
    inside = (lane >= start) & (lane < start + PIVOT)
    pivot = invert_small(rows[:, start : start + PIVOT])
    unit = jnp.where(lane - start == line, 1.0, 0.0)
    high, middle, low = split_three(jnp.where(inside, unit, rows))
    p_high, p_middle, p_low = split_three(pivot)
    new_rows = jnp.dot(
        jnp.concatenate([p_high, p_high, p_middle, p_high, p_middle, p_low], axis=1),
        jnp.concatenate([high, middle, high, low, middle, high], axis=0),
        preferred_element_type=jnp.float32,
    )
    c_high, c_middle, c_low = split_three(jnp.where(lane < start, -rows, rows))
    high, middle, low = split_three(new_rows)
    left = jnp.concatenate([c_high, c_high, c_middle, c_high, c_middle, c_low], axis=0)
    right = jnp.concatenate([high, middle, high, low, middle, high], axis=0)

    def change(part):
        return lax.dot_general(
            part, right, (((0,), (0,)), ((), ())), preferred_element_type=jnp.float32
        )

    after = start + PIVOT
    next_rows = None
    if after < size:
        next_rows = jnp.where(inside, 0.0, matrix[after : after + PIVOT]) - change(
            left[:, after : after + PIVOT]
        )
    lane_all = lax.broadcasted_iota(jnp.int32, (size, size), 1)
    inside_all = (lane_all >= start) & (lane_all < after)
    rest = jnp.where(inside_all, 0.0, matrix) - change(left)
    pieces = [rest[:start], new_rows, rest[after:]]
    matrix = jnp.concatenate([piece for piece in pieces if piece.shape[0]], axis=0)
    return matrix, next_rows


def add_squares(squares, mixed, values):
    high, middle = split(values)
    contract = (((0,), (0,)), ((), ()))
    both = lax.dot_general(
        high, jnp.concatenate([high, middle], axis=1), contract, preferred_element_type=jnp.float32
    )
    rest = lax.dot_general(middle, middle, contract, preferred_element_type=jnp.float32)
    width = values.shape[1]
    squares[...] += both[:, :width] + rest
    mixed[...] += both[:, width:]


def kernel(
    n_row,
    n_col,
    row_most,
    count_ref,
    owner_ref,
    second_ref,
    third_ref,
    target_col_ref,
    target_ref,
    x_hbm,
    b_hbm,
    c_hbm,
    out_ref,
    lists,
    index_ref,
    x_ref,
    b_all,
    b_now,
    c_ref,
    c_high,
    c_low,
    gram2,
    gram3,
    mixed,
    gram_in,
    normal_in,
    partials,
    send,
    arrive,
    load_sem,
    line_send,
    line_recv,
    pair_send,
    pair_recv,
    gram_send,
    gram_recv,
    normal_send,
    normal_recv,
    block_send,
    block_recv,
):
    row = lax.axis_index("row")
    col = lax.axis_index("col")
    chip, core = row // 2, row % 2
    chips = n_row // 2
    other = chip * 2 + 1 - core
    edge = x_ref.shape[1]
    slots = lists.shape[0]
    per_row = row_most
    rank = c_ref.shape[1]
    piece = rank // n_row
    rows_out = IB_DEV * edge
    held_blocks = b_hbm.shape[0]
    own_blocks = pl.ds(row * held_blocks, held_blocks)

    load_b = pltpu.make_async_copy(b_hbm, b_all.at[own_blocks], load_sem.at[0])
    load_c = pltpu.make_async_copy(c_hbm, c_ref, load_sem.at[1])
    load_x = pltpu.make_async_copy(x_hbm, x_ref, load_sem.at[2])
    load_b.start()
    load_c.start()
    load_x.start()

    barrier = pltpu.get_barrier_semaphore()
    for step in range(1, n_row):
        pl.semaphore_signal(
            barrier, inc=1, device_id=((row + step) % n_row, col), device_id_type=MESH
        )
    for step in range(1, n_col):
        pl.semaphore_signal(
            barrier, inc=1, device_id=(row, (col + step) % n_col), device_id_type=MESH
        )
    tiles = owner_ref.shape[1]
    tile_line = lax.broadcasted_iota(jnp.int32, (tiles, tiles), 0)
    tile_lane = lax.broadcasted_iota(jnp.int32, (tiles, tiles), 1)
    owner = owner_ref[...]
    owner_line = jnp.sum(
        jnp.where(tile_line == tile_lane, owner, 0), axis=1, keepdims=True, dtype=jnp.int32
    )
    before = (owner_line == owner) & (tile_line < tile_lane)
    place = owner * row_most + jnp.sum(
        jnp.where(before, 1, 0), axis=0, keepdims=True, dtype=jnp.int32
    )
    taken = lax.broadcasted_iota(jnp.int32, (slots, tiles), 0) == place
    number = lax.broadcasted_iota(jnp.int32, (1, tiles), 1)
    code = jnp.where(number < count_ref[0], target_col_ref[...] * IB_DEV + target_ref[...] + 1, 0)
    list_lane = lax.broadcasted_iota(jnp.int32, lists.shape, 1)
    table = jnp.zeros(lists.shape, jnp.int32)
    for which, values in enumerate((number, second_ref[...], third_ref[...], code)):
        listed = jnp.sum(jnp.where(taken, values, 0), axis=1, keepdims=True, dtype=jnp.int32)
        table = jnp.where(list_lane == which, listed, table)
    lists[...] = table
    load_lists = pltpu.make_async_copy(lists, index_ref, load_sem.at[3])
    load_lists.start()

    load_b.wait()
    pl.semaphore_wait(barrier, n_row + n_col - 2)

    def line_copy(way, step, slot_chip, to_chip):
        held = pl.ds((slot_chip * 2 + core) * held_blocks, held_blocks)
        return pltpu.make_async_remote_copy(
            src_ref=b_all.at[held],
            dst_ref=b_all.at[held],
            send_sem=line_send.at[way, step],
            recv_sem=line_recv.at[way, step],
            device_id=(to_chip * 2 + core, col),
            device_id_type=MESH,
        )

    def pair_copy(number, slot_row):
        held = pl.ds(slot_row * held_blocks, held_blocks)
        return pltpu.make_async_remote_copy(
            src_ref=b_all.at[held],
            dst_ref=b_all.at[held],
            send_sem=pair_send.at[number],
            recv_sem=pair_recv.at[number],
            device_id=(other, col),
            device_id_type=MESH,
        )

    def has(way, step):
        return chip >= 1 + step if way == 0 else chip + 1 + step < chips

    def sends(way, step):
        if way == 0:
            return (chip < chips - 1) & (chip >= step)
        return (chip > 0) & (chip + step < chips)

    def sent_chip(way, step):
        return chip - step if way == 0 else chip + step

    def next_chip(way):
        return chip + 1 if way == 0 else chip - 1

    for way in range(2):

        @pl.when(sends(way, 0))
        def _():
            line_copy(way, 0, sent_chip(way, 0), next_chip(way)).start()

    pair_copy(0, row).start()

    load_c.wait()
    third = c_ref[...]
    high, low = split(third)
    c_high[...] = high.reshape(c_high.shape)
    c_low[...] = low.reshape(c_low.shape)
    gram3[...] = jnp.zeros_like(gram3)
    mixed[...] = jnp.zeros_like(mixed)
    add_squares(gram3, mixed, third)
    gram3[...] += mixed[...] + mixed[...].T
    gram2[...] = jnp.zeros_like(gram2)
    mixed[...] = jnp.zeros_like(mixed)
    load_x.wait()
    load_lists.wait()
    lane = lax.broadcasted_iota(jnp.int32, (edge, 128), 1)
    lane_row = lax.broadcasted_iota(jnp.int32, (1, 128), 1) // edge
    one_mask = [jnp.where(lane_row == m, 1.0, 0.0).astype(jnp.bfloat16) for m in range(4)]
    two_mask = [jnp.where(lane_row % 2 == m, 1.0, 0.0).astype(jnp.bfloat16) for m in range(2)]
    chunks = edge * edge // 128

    def tile(slot, second):
        third_at = index_ref[slot, 2]
        tile_at = index_ref[slot, 0]
        weights = jnp.concatenate([c_high[third_at]] * 6 + [c_low[third_at]] * 2, axis=0)
        total = None
        for part in range(2):
            pieces = []
            for q in range(part * chunks // 2, (part + 1) * chunks // 2):
                x = x_ref[tile_at, :, q * 128 : (q + 1) * 128]
                first = x.astype(jnp.bfloat16)
                x_high = first.astype(jnp.float32)
                x_low = x - x_high
                turned_high = pltpu.roll(x_high, 64, 1)
                turned_low = pltpu.roll(x_low, 64, 1)
                front = jnp.where(lane < 64, x_low, turned_high).astype(jnp.bfloat16)
                back = jnp.where(lane < 64, turned_low, x_high).astype(jnp.bfloat16)
                for m in range(4):
                    rest = front if m < 2 else back
                    pieces.append(
                        jnp.concatenate([first * one_mask[m], rest * two_mask[m % 2]], axis=1)
                    )
            inner = jnp.dot(
                jnp.concatenate(pieces, axis=0), weights, preferred_element_type=jnp.float32
            )
            for at in range(edge // 2):
                j = part * edge // 2 + at
                term = inner[at * edge : (at + 1) * edge] * second[j : j + 1]
                total = term if total is None else total + term
        partials[:, pl.ds(slot, 1), :] = total[:, None, :]

    def use(held_chip):
        for side in range(2):
            held = b_all[pl.ds((held_chip * 2 + side) * held_blocks, held_blocks)]
            b_now[side] = held
            flat = held.reshape(held_blocks * edge, rank)
            add_squares(gram2, mixed, flat)

    def tiles_of(held_chip):
        def pair(s, carried):
            for side in range(2):
                slot = (held_chip * 2 + side) * per_row + s
                tile(slot, b_now[side, index_ref[slot, 1]])
            return carried

        lax.fori_loop(0, per_row, pair, 0)

    def gram_copy(step, which):
        to_col = (col + step) % n_col
        source = gram2 if which == 0 else gram3
        return pltpu.make_async_remote_copy(
            src_ref=source.at[pl.ds(pl.multiple_of(row * piece, 8), piece)],
            dst_ref=gram_in.at[which, step],
            send_sem=gram_send.at[which, step],
            recv_sem=gram_recv.at[which, step],
            device_id=(row, to_col),
            device_id_type=MESH,
        )

    nearer = jnp.minimum(chip, chips - 1 - chip)

    def turn(number, carried):
        step = number - 1
        for way in range(2):

            @pl.when((number > 0) & has(way, step))
            def _():
                held = sent_chip(way, step + 1)
                line_copy(way, step, held, next_chip(way)).wait_recv()

                @pl.when((step + 1 < chips - 1) & sends(way, step + 1))
                def _():
                    line_copy(way, step + 1, held, next_chip(way)).start()

                pair_copy(1 + 2 * step + way, held * 2 + core).start()

        both = jnp.where(number % 2 == 1, chip - (number + 1) // 2, chip + number // 2)
        one = jnp.where(
            chip < chips - 1 - chip, chip + number - nearer, chip - number + nearer
        )
        held = jnp.where(number <= 2 * nearer, both, one)
        pair_at = jnp.where(held < chip, 2 * (chip - held) - 1, 2 * (held - chip))
        pair_copy(pair_at, held * 2 + 1 - core).wait_recv()
        use(held)

        @pl.when(number == chips - 1)
        def _():
            gram2[...] += mixed[...] + mixed[...].T
            for to_step in range(1, n_col):
                gram_copy(to_step, 0).start()
                gram_copy(to_step, 1).start()

        tiles_of(held)
        return carried

    lax.fori_loop(0, chips, turn, 0)

    for step in range(1, n_col):
        gram_copy(step, 0).wait_recv()
        gram_copy(step, 1).wait_recv()
    own_piece = pl.ds(pl.multiple_of(row * piece, 8), piece)
    sum2, sum3 = gram2[own_piece, :], gram3[own_piece, :]
    for step in range(1, n_col):
        sum2 = sum2 + gram_in[0, step]
        sum3 = sum3 + gram_in[1, step]
    normal_in[row] = sum2 * sum3

    def normal_copy(step, slot):
        return pltpu.make_async_remote_copy(
            src_ref=normal_in.at[slot],
            dst_ref=normal_in.at[slot],
            send_sem=normal_send.at[step],
            recv_sem=normal_recv.at[step],
            device_id=((row + step) % n_row, col),
            device_id_type=MESH,
        )

    for step in range(1, n_row):
        normal_copy(step, row).start()

    targets = n_col * IB_DEV
    code_line = lists[:, 3:4]
    same = lax.broadcasted_iota(jnp.int32, (slots, slots), 0) == lax.broadcasted_iota(
        jnp.int32, (slots, slots), 1
    )
    code_lane = jnp.sum(jnp.where(same, code_line, 0), axis=0, keepdims=True, dtype=jnp.int32)
    chosen = lax.broadcasted_iota(jnp.int32, (targets, slots), 0) + 1 == code_lane
    chosen = jnp.where(chosen, 1.0, 0.0)
    chosen = jnp.concatenate([chosen, chosen], axis=1).astype(jnp.bfloat16)

    live = code_line > 0

    def block_copy(number, source, target, to_col):
        return pltpu.make_async_remote_copy(
            src_ref=source,
            dst_ref=target,
            send_sem=block_send.at[number],
            recv_sem=block_recv.at[number],
            device_id=(row, to_col),
            device_id_type=MESH,
        )

    def choose(group, carried):
        for part in range(4):
            i = group * 4 + part
            high, low = split(jnp.where(live, partials[i], 0.0))
            rows = jnp.dot(
                chosen, jnp.concatenate([high, low], axis=0), preferred_element_type=jnp.float32
            )
            for c in range(n_col):
                send[c, pl.ds(pl.multiple_of(i * IB_DEV, IB_DEV), IB_DEV), :] = rows[
                    c * IB_DEV : (c + 1) * IB_DEV
                ]
        return carried

    lines = edge // PIECES
    length = lines * IB_DEV
    pieces = [pl.ds(number * length, length) for number in range(PIECES)]
    corners, beside, later = [], [], []
    if n_col == 4:
        near = (col // 2) * 2 + 1 - col % 2
        far = (1 - col // 2) * 2 + col % 2
        corner = (1 - col // 2) * 2 + 1 - col % 2
        sides = (near, far)
        for number, held in enumerate(pieces):
            first, second = sides[number % 2], sides[1 - number % 2]
            corners.append(block_copy(number, send.at[corner, held], arrive.at[0, held], first))
            beside.append(
                block_copy(PIECES + number, send.at[first, held], arrive.at[1, held], first)
            )
            later.append(
                block_copy(2 * PIECES + number, send.at[second, held], arrive.at[2, held], second)
            )
    else:
        for step in range(1, n_col):
            to_col = (col + step) % n_col
            beside.append(block_copy(step - 1, send.at[to_col], arrive.at[step - 1], to_col))
    for number in range(PIECES):
        lax.fori_loop(number * lines // 4, (number + 1) * lines // 4, choose, 0)
        if corners:
            corners[number].start()
    for copy in beside:
        copy.start()

    for step in range(1, n_row):
        normal_copy(step, (row + n_row - step) % n_row).wait_recv()
    matrix = jnp.concatenate([normal_in[r] for r in range(n_row)], axis=0)
    pivots = rank // PIVOT
    rows = matrix[:PIVOT]
    for at in range(pivots):
        matrix, rows = eliminate(matrix, rows, at)
        for number in range(len(later)):
            if at == (1 + 2 * (number // 2)) * pivots // 8:
                held, second = pieces[number], sides[1 - number % 2]
                corners[number].wait_recv()
                send[second, held] += arrive[0, held]
                later[number].start()

    if not later:
        for copy in beside:
            copy.wait_recv()
    for number, held in enumerate(pieces):
        total = send[col, held]
        if later:
            beside[number].wait_recv()
            later[number].wait_recv()
            total = total + arrive[1, held] + arrive[2, held]
        else:
            for step in range(n_col - 1):
                total = total + arrive[step, held]
        solved = exact_dot(total, matrix)
        for i in range(lines):
            out_ref[:, pl.ds(number * lines + i, 1), :] = solved[
                i * IB_DEV : (i + 1) * IB_DEV
            ][:, None, :]

    for copy in corners + beside + later:
        copy.wait_send()
    for step in range(1, n_row):
        normal_copy(step, row).wait_send()
    for step in range(1, n_col):
        gram_copy(step, 0).wait_send()
        gram_copy(step, 1).wait_send()
    pair_copy(0, row).wait_send()
    for step in range(chips - 1):
        for way in range(2):

            @pl.when(has(way, step))
            def _():
                pair_copy(1 + 2 * step + way, sent_chip(way, step + 1) * 2 + core).wait_send()

            @pl.when(sends(way, step))
            def _():
                line_copy(way, step, sent_chip(way, step), next_chip(way)).wait_send()


def local(
    n_row,
    n_col,
    tile_values,
    tile_count,
    mode1_column,
    mode1_offset,
    mode2_row,
    mode2_offset,
    mode3_offset,
    mode2_factor,
    mode3_factor,
):
    slots, edge = tile_values.shape[0], tile_values.shape[1]
    rows_held, rank = mode2_factor.shape
    blocks_held = rows_held // edge
    row_most = {8: 7, 16: 4}.get(n_row, slots)
    places = n_row * row_most
    lists = [
        values.reshape(1, slots)
        for values in (mode2_row, mode2_offset, mode3_offset, mode1_column, mode1_offset)
    ]
    rows_out = IB_DEV * edge
    piece = rank // n_row
    chips = n_row // 2
    f32, bf16 = jnp.float32, jnp.bfloat16
    dma = pltpu.SemaphoreType.DMA
    vmem = pl.BlockSpec(memory_space=pltpu.VMEM)
    smem = pl.BlockSpec(memory_space=pltpu.SMEM)
    hbm = pl.BlockSpec(memory_space=pltpu.HBM)
    blocks = max(3 * PIECES, n_col - 1)
    out = pl.pallas_call(
        functools.partial(kernel, n_row, n_col, row_most),
        out_shape=jax.ShapeDtypeStruct((IB_DEV, edge, rank), f32),
        in_specs=[smem] + [vmem] * 5 + [hbm, hbm, hbm],
        out_specs=vmem,
        scratch_shapes=[
            pltpu.VMEM((places, 128), jnp.int32),
            pltpu.SMEM((places, 128), jnp.int32),
            pltpu.VMEM(tile_values.shape, f32),
            pltpu.VMEM((n_row * blocks_held, edge, rank), f32),
            pltpu.VMEM((2, blocks_held, edge, rank), f32),
            pltpu.VMEM(mode3_factor.shape, f32),
            pltpu.VMEM((mode3_factor.shape[0] // edge, edge, rank), bf16),
            pltpu.VMEM((mode3_factor.shape[0] // edge, edge, rank), bf16),
            pltpu.VMEM((rank, rank), f32),
            pltpu.VMEM((rank, rank), f32),
            pltpu.VMEM((rank, rank), f32),
            pltpu.VMEM((2, n_col, piece, rank), f32),
            pltpu.VMEM((n_row, piece, rank), f32),
            pltpu.VMEM((edge, places, rank), f32),
            pltpu.VMEM((n_col, rows_out, rank), f32),
            pltpu.VMEM((max(3, n_col - 1), rows_out, rank), f32),
            dma((4,)),
            dma((2, chips)),
            dma((2, chips)),
            dma((2 * chips,)),
            dma((2 * chips,)),
            dma((2, n_col)),
            dma((2, n_col)),
            dma((n_row,)),
            dma((n_row,)),
            dma((blocks,)),
            dma((blocks,)),
        ],
        compiler_params=pltpu.CompilerParams(
            collective_id=0, has_side_effects=True, vmem_limit_bytes=60 * 2**20
        ),
    )(tile_count, *lists, tile_values, mode2_factor.reshape(blocks_held, edge, rank), mode3_factor)
    return out.reshape(rows_out, rank)


def solution(mesh):
    placed = (
        P(("row", "col"), None, None),
        P(("row", "col")),
        P(("row", "col"), None),
        P(("row", "col")),
        P(("row", "col"), None),
        P(("row", "col")),
        P(("row", "col")),
        P(("row", "col"), None),
        P("col", None),
    )
    return jax.shard_map(
        functools.partial(local, mesh.shape["row"], mesh.shape["col"]),
        mesh=mesh,
        in_specs=placed,
        out_specs=P(("row", "col"), None),
        check_vma=False,
    )
```
